512 devices in a mesh: section: 8 (over z_lo), node: 2 (over core), local: 32 (over z_hi, x, y).
Axes of the slice: x: 4, y: 4, z: 16 (z_hi: 2, z_lo: 8; z = z_hi * 8 + z_lo), core: 2. Of those that a mesh axis runs over, the one named last changes fastest.
Arguments:
- act_forward: bfloat16 [32768, 2048], P(('section', 'local'), 'node'), may hold values from -6 to 6
- routes_forward: int32 [32768, 6], P(('section', 'local')), may hold values from 0 to 31, all different within a row; in each aligned block of 128 rows (0 to 127, 128 to 255, ...) at most 25 rows name the same one
- gates_forward: bfloat16 [32768, 6], P(('section', 'local')), may hold values from 0.049804688 to 1
- act_backward: bfloat16 [32768, 2048], P(('section', 'local'), 'node'), may hold values from -6 to 6
- grad_backward: bfloat16 [32768, 2048], P(('section', 'local'), 'node'), may hold values from -6 to 6
- routes_backward: int32 [32768, 6], P(('section', 'local')), may hold values from 0 to 31, all different within a row; in each aligned block of 128 rows (0 to 127, 128 to 255, ...) at most 25 rows name the same one
- gates_backward: bfloat16 [32768, 6], P(('section', 'local')), may hold values from 0.049804688 to 1
- w_in: bfloat16 [8, 32, 2048, 768], P('section', 'local', 'node'), may hold values from -0.125 to 0.125
- w_out: bfloat16 [8, 32, 768, 2048], P('section', 'local', None, 'node'), may hold values from -0.21875 to 0.21875
Outputs:
- sent_forward: bfloat16 [32768, 2048], P(('section', 'local'), 'node')
- sent_backward: bfloat16 [32768, 2048], P(('section', 'local'), 'node')
The draws below stay inside these ranges and needn't reach their ends.
Inputs may be any that keep to these rules, and one draw needn't show every extreme that they name: `routes_forward`: each token names 6 different experts. In each aligned block of 128 rows no expert is named by more than 25 rows, a bound that some block reaches. `routes_backward`: as for routes_forward.
All inputs are finite; a program needn't handle non-finite values.
Results may differ from the reference program's by a relative error of at most 0.019.
Values may be sent and summed in bfloat16 or wider, within the bound.
No kernel may reach another device: no remote copies, remote signals or barrier semaphores. Data moves between devices by JAX's collectives and lax.ppermute only.
A program may use at most 64 MiB of HBM per device.

```python
import math
import jax
import jax.numpy as jnp
import numpy as np
from jax import lax

D = 2048
HID = 768
TOP = 6
TOK_DEV = 128
EXPERTS = 32
CAP = 25
SECTIONS = 8
TOKENS = 32768
N_SECTION = 8
N_NODE = 2
N_LOCAL = 32


def level_of(rng, dims, cuts, least, top_value):
    factor_of = 1.0
    for dim, parts in cuts:
        heights = jax.random.uniform(jax.random.fold_in(jax.random.fold_in(rng, 6), dim), (parts,), jnp.float32, least / len(cuts), top_value / len(cuts))
        factor_of = factor_of * jnp.repeat(jnp.exp(heights), dims[dim] // parts).reshape((-1,) + (1,) * (len(dims) - 1 - dim))
    return factor_of


def routed_block(key, own, number, rows, number_of, top, reach, lean):
    order = jax.random.permutation(key, number_of)
    packed, ordinary = shares(number_of, rows * top, reach, lean, True), shares(number_of, rows * top, reach, lean, False)
    places = jnp.arange(number_of)

    def named(tallies, offset_by):
        used = int((tallies > 0).sum())
        fixed = max(1, used // 4)
        moved = fixed + (places - fixed + offset_by * (used - fixed)) % max(1, number_of - fixed)
        return jnp.zeros((number_of,), jnp.int32).at[order[jnp.where(places < fixed, places, moved)]].set(jnp.asarray(tallies, jnp.int32))

    tallies = jnp.where(number % 4 == 0, named(packed, number // 4), named(ordinary, number - number // 4 - 1))
    mixed = jax.random.permutation(jax.random.fold_in(own, 3), number_of)
    donor, receiver = mixed[0:number_of // 2 * 2:2], mixed[1:number_of // 2 * 2:2]
    slack = jnp.minimum(tallies[donor] - 1, reach - tallies[receiver]) // 2
    slack = jnp.where((donor == order[0]) | (receiver == order[0]) | (tallies[receiver] == 0), 0, jnp.maximum(slack, 0))
    moved = jax.random.randint(jax.random.fold_in(own, 4), (number_of // 2,), 0, 1 << 20) % (slack + 1)
    tallies = tallies.at[donor].add(-moved).at[receiver].add(moved)
    members = jnp.searchsorted(jnp.cumsum(tallies), jnp.arange(rows * top), side="right").astype(jnp.int32)
    table = members.reshape(top, rows).T
    table = table[jax.random.permutation(jax.random.fold_in(own, 1), rows)]
    offset_by = jax.random.randint(jax.random.fold_in(own, 2), (rows, 1), 0, top)
    return jnp.take_along_axis(table, (jnp.arange(top)[None, :] + offset_by) % top, axis=1)


def shares(number_of, total, limit, lean, full):
    portions = [(1 << 20) // math.isqrt(grade ** lean) + 1 for grade in range(1, number_of + 1)]
    largest = limit if full else min(limit, max(-(-total // number_of), total * portions[0] // sum(portions)))
    least = 1 if total - largest >= number_of - 1 else 0
    holding, surplus = [largest] + [least] * (number_of - 1), total - largest - least * (number_of - 1)
    while surplus > 0:
        movable = [i for i in range(1, number_of) if holding[i] < largest] or [i for i in range(1, number_of) if holding[i] < limit]
        whole, budget = sum([portions[i] for i in movable]), surplus
        for i in movable:
            more = min(limit - holding[i], max(1, budget * portions[i] // whole), surplus)
            holding[i] = holding[i] + more
            surplus = surplus - more
    return np.array(holding)


def normal_values(rng, dims, width, reach, shards=(), held_as=jnp.bfloat16):
    level = level_of(rng, dims, shards, -0.22, 0.18) if shards else 1.0
    values = jax.random.normal(rng, dims, jnp.float32) * width * level
    return jnp.minimum(jnp.maximum(values, -reach), reach).astype(held_as)


def setup_inputs(seed: int = 0) -> dict:
    keys = jax.random.split(jax.random.key(seed), 10)
    act_forward = normal_values(keys[0], (TOKENS, D), 1.0, 6.0, ((0, 256), (1, 2)))
    routes_forward_keys = jax.random.split(jax.random.fold_in(keys[1], 1), TOKENS // TOK_DEV)
    routes_forward_turns = jax.random.permutation(jax.random.fold_in(keys[1], 3), TOKENS // TOK_DEV)
    routes_forward = jax.vmap(lambda own, number: routed_block(jax.random.fold_in(keys[1], 2), own, number, TOK_DEV, EXPERTS, TOP, CAP, 2))(routes_forward_keys, routes_forward_turns).reshape((TOKENS, TOP))
    gates_forward = jnp.clip(jnp.exp(math.log(1.0) - 2.9996462 * jax.random.uniform(keys[2], (TOKENS, TOP), jnp.float32) ** level_of(keys[2], (TOKENS, TOP), ((0, 256),), -0.2, 0.2)), 0.049804688, 1.0).astype(jnp.bfloat16)
    act_backward = normal_values(keys[3], (TOKENS, D), 1.0, 6.0, ((0, 256), (1, 2)))
    grad_backward = normal_values(keys[4], (TOKENS, D), 1.0, 6.0, ((0, 256), (1, 2)))
    routes_backward_keys = jax.random.split(jax.random.fold_in(keys[5], 1), TOKENS // TOK_DEV)
    routes_backward_turns = jax.random.permutation(jax.random.fold_in(keys[5], 3), TOKENS // TOK_DEV)
    routes_backward = jax.vmap(lambda own, number: routed_block(jax.random.fold_in(keys[5], 2), own, number, TOK_DEV, EXPERTS, TOP, CAP, 2))(routes_backward_keys, routes_backward_turns).reshape((TOKENS, TOP))
    gates_backward = jnp.clip(jnp.exp(math.log(1.0) - 2.9996462 * jax.random.uniform(keys[6], (TOKENS, TOP), jnp.float32) ** level_of(keys[6], (TOKENS, TOP), ((0, 256),), -0.2, 0.2)), 0.049804688, 1.0).astype(jnp.bfloat16)
    w_in = normal_values(keys[7], (SECTIONS, EXPERTS, D, HID), D ** -0.5, 0.125, ((0, 8), (1, 32), (2, 2)))
    w_out = normal_values(keys[8], (SECTIONS, EXPERTS, HID, D), HID ** -0.5, 0.21875, ((0, 8), (1, 32), (3, 2)))
    return dict(act_forward=act_forward, routes_forward=routes_forward, gates_forward=gates_forward, act_backward=act_backward, grad_backward=grad_backward, routes_backward=routes_backward, gates_backward=gates_backward, w_in=w_in, w_out=w_out)


def destinations(route_ids):
    block_count = route_ids.shape[0]
    flat_ids = route_ids.reshape(block_count, TOK_DEV * TOP)
    labels = jnp.arange(EXPERTS, dtype=jnp.int32)
    onehot = (flat_ids[:, :, None] == labels[None, None, :]).astype(jnp.int32)
    before = jnp.cumsum(onehot, axis=1) - onehot
    ranking = jnp.sum(before * onehot, axis=2).astype(jnp.int32)
    return (flat_ids * CAP + ranking).reshape(block_count, TOK_DEV, TOP).astype(jnp.int32)


def token_table(target):
    block_count = target.shape[0]
    table = jnp.full((block_count, EXPERTS * CAP), TOK_DEV, dtype=jnp.int32)
    block_ids = jnp.broadcast_to(jnp.arange(block_count, dtype=jnp.int32)[:, None, None], target.shape)
    token_ids = jnp.broadcast_to(jnp.arange(TOK_DEV, dtype=jnp.int32)[None, :, None], target.shape)
    table = table.at[block_ids, target].set(token_ids)
    return jnp.transpose(table.reshape(block_count, EXPERTS, CAP), (1, 0, 2))


def split_sum(rows, weight):
    count = rows.shape[0]
    pieces = rows.reshape(count, N_NODE, -1).astype(jnp.float32)
    blocks = weight.reshape(N_NODE, -1, weight.shape[1]).astype(jnp.float32)
    partial_terms = jnp.einsum("rnd,ndh->rnh", pieces, blocks).astype(jnp.bfloat16)
    partial_terms = lax.optimization_barrier(partial_terms)
    return jnp.sum(partial_terms.astype(jnp.float32), axis=1)


def combine(results, target, gates):
    block_count = target.shape[0]
    block_ids = jnp.arange(block_count, dtype=jnp.int32)[:, None]
    total = jnp.zeros((block_count, TOK_DEV, D), jnp.float32)
    for pick in range(TOP):
        picked = results[block_ids, target[:, :, pick]]
        total = total + gates[:, :, pick, None].astype(jnp.float32) * picked.astype(jnp.float32)
    return total.astype(jnp.bfloat16)


def section_pass(inputs):
    act_f, ids_f, gate_f, act_b, grad_b, ids_b, gate_b, weights_in, weights_out = inputs
    shape3 = (N_LOCAL, TOK_DEV, TOP)
    target_f = destinations(ids_f.reshape(shape3))
    target_b = destinations(ids_b.reshape(shape3))
    table_f = token_table(target_f)
    table_b = token_table(target_b)
    zero_row = jnp.zeros((N_LOCAL, 1, D), jnp.bfloat16)
    padded_f = jnp.concatenate([act_f.reshape(N_LOCAL, TOK_DEV, D), zero_row], axis=1)
    padded_b = jnp.concatenate([act_b.reshape(N_LOCAL, TOK_DEV, D), zero_row], axis=1)
    padded_g = jnp.concatenate([grad_b.reshape(N_LOCAL, TOK_DEV, D), zero_row], axis=1)
    block_ids = jnp.arange(N_LOCAL, dtype=jnp.int32)[:, None]

    def per_expert(item):
        weight_in, weight_out, slots_f, slots_b = item
        rows_f = padded_f[block_ids, slots_f].reshape(N_LOCAL * CAP, D)
        hidden = jax.nn.silu(split_sum(rows_f, weight_in)).astype(jnp.bfloat16)
        out_f = jnp.dot(hidden, weight_out, preferred_element_type=jnp.float32).astype(jnp.bfloat16)
        rows_b = padded_b[block_ids, slots_b].reshape(N_LOCAL * CAP, D)
        rows_g = padded_g[block_ids, slots_b].reshape(N_LOCAL * CAP, D)
        preact = split_sum(rows_b, weight_in)
        back_h = split_sum(rows_g, weight_out.T)
        sigma = 1.0 / (1.0 + jnp.exp(-preact))
        grad_hidden = (back_h * sigma * (1.0 + preact * (1.0 - sigma))).astype(jnp.bfloat16)
        out_b = jnp.dot(grad_hidden, weight_in.T, preferred_element_type=jnp.float32).astype(jnp.bfloat16)
        return out_f, out_b

    outs_f, outs_b = lax.map(per_expert, (weights_in, weights_out, table_f, table_b))

    def arrange(results):
        results = results.reshape(EXPERTS, N_LOCAL, CAP, D)
        return jnp.transpose(results, (1, 0, 2, 3)).reshape(N_LOCAL, EXPERTS * CAP, D)

    layer_out = combine(arrange(outs_f), target_f, gate_f.reshape(shape3))
    input_grad = combine(arrange(outs_b), target_b, gate_b.reshape(shape3))
    return layer_out.reshape(N_LOCAL * TOK_DEV, D), input_grad.reshape(N_LOCAL * TOK_DEV, D)


def reference(act_forward, routes_forward, gates_forward, act_backward, grad_backward, routes_backward, gates_backward, w_in, w_out):
    rows = N_LOCAL * TOK_DEV

    def sectioned(array):
        return array.reshape((N_SECTION, rows) + array.shape[1:])

    layer_out, input_grad = lax.map(section_pass, (sectioned(act_forward), sectioned(routes_forward), sectioned(gates_forward), sectioned(act_backward), sectioned(grad_backward), sectioned(routes_backward), sectioned(gates_backward), w_in, w_out))
    sent_forward = jnp.roll(layer_out, 1, axis=0).reshape(TOKENS, D)
    sent_backward = jnp.roll(input_grad, -1, axis=0).reshape(TOKENS, D)
    return (sent_forward, sent_backward)
```

```python
import jax
import jax.numpy as jnp
from jax import lax
from jax.sharding import Mesh, PartitionSpec as P

CAP = 25
NODE = "node"
PLANE = ("x", "y")
RING = ("section", "zhi", "x", "y")


def pairs_of(shape, move):
    sections, halves, xs, ys = shape
    pairs = []
    for s in range(sections):
        for h in range(halves):
            for x in range(xs):
                for y in range(ys):
                    s2, h2 = move(s, h)
                    src = ((s * halves + h) * xs + x) * ys + y
                    dst = ((s2 * halves + h2) * xs + x) * ys + y
                    pairs.append((src, dst))
    return pairs


def moved(v, by, cross):
    shape = tuple(lax.axis_size(a) for a in RING)
    sections = shape[0]
    return lax.ppermute(
        v, RING, pairs_of(shape, lambda s, h: ((s + by) % sections, 1 - h if cross else h))
    )


def other_core(v):
    return lax.ppermute(v, NODE, [(0, 1), (1, 0)])


def exchange(v):
    return lax.all_to_all(v, PLANE, split_axis=0, concat_axis=0, tiled=True)


def note_of(routes, gates, width):
    note = jnp.concatenate([routes.astype(jnp.bfloat16).T, gates.T], axis=0)
    return jnp.pad(note, ((0, 16 - note.shape[0]), (0, width - note.shape[1])))


def tables(routes, gates, first, experts, rows):
    top, tokens = routes.shape
    half = tokens // 2
    labels = first + jnp.arange(experts, dtype=jnp.int32)
    match = routes[:, None, :] == labels[None, :, None]
    chosen = jnp.sum(match.astype(jnp.float32), axis=0)
    weight = jnp.sum(jnp.where(match, gates.astype(jnp.float32)[:, None, :], 0.0), axis=0)
    at = jnp.arange(tokens, dtype=jnp.int32)
    earlier = (at[:, None] < at[None, :]) & ((at[:, None] // half) == (at[None, :] // half))
    rank = jnp.dot(
        chosen.astype(jnp.bfloat16), earlier.astype(jnp.bfloat16), preferred_element_type=jnp.float32
    )
    place = jnp.where(chosen > 0, rank.astype(jnp.int32) + CAP * (at // half)[None, :], -1)
    hit = place[:, None, :] == jnp.arange(rows, dtype=jnp.int32)[None, :, None]
    send = hit.astype(jnp.bfloat16).reshape(experts * rows, tokens)
    mix = jnp.where(hit, weight[:, None, :], 0.0).astype(jnp.bfloat16).reshape(experts * rows, tokens)
    return send, mix


def dot32(a, b, dims=(((1,), (0,)), ((), ()))):
    return lax.dot_general(a, b, dims, preferred_element_type=jnp.float32)


def local(
    act_forward,
    routes_forward,
    gates_forward,
    act_backward,
    grad_backward,
    routes_backward,
    gates_backward,
    w_in,
    w_out,
):
    weight_in = w_in[0, 0]
    weight_out = w_out[0, 0]
    tok, cols = act_forward.shape
    top = routes_forward.shape[1]
    experts = lax.axis_size("x") * lax.axis_size("y")
    rows = (2 * CAP + 7) // 8 * 8
    first = lax.axis_index("zhi") * experts
    bf = jnp.bfloat16

    note_f = note_of(routes_forward, gates_forward, cols)
    note_b = note_of(routes_backward, gates_backward, cols)
    far_f = moved(jnp.concatenate([act_forward, note_f], axis=0), 0, True)
    far_a = moved(jnp.concatenate([act_backward, note_b], axis=0), 0, True)
    far_g = moved(grad_backward, 0, True)

    def both_tables(note, far):
        far_note = far[tok:]
        joined = jnp.concatenate([note[: 2 * top, :tok], far_note[: 2 * top, :tok]], axis=1)
        return tables(
            joined[:top].astype(jnp.int32), joined[top:], first, experts, rows
        )

    send_f, mix_f = both_tables(note_f, far_f)
    send_b, mix_b = both_tables(note_b, far_a)

    def pack(send, near, far):
        return dot32(send, jnp.concatenate([near, far[:tok]], axis=0)).astype(bf).reshape(
            experts, rows, cols
        )

    got_f = exchange(pack(send_f, act_forward, far_f)).reshape(-1, cols)
    got_a = exchange(pack(send_b, act_backward, far_a)).reshape(-1, cols)
    got_g = exchange(pack(send_b, grad_backward, far_g)).reshape(-1, cols)

    part = dot32(got_f, weight_in).astype(bf)
    pre = part.astype(jnp.float32) + other_core(part).astype(jnp.float32)
    hidden = jax.nn.silu(pre).astype(bf)
    out_f = dot32(hidden, weight_out).astype(bf).reshape(experts, rows, cols)
    back_f = exchange(out_f).reshape(-1, cols)

    contract = (((1,), (1,)), ((), ()))
    part_pre = dot32(got_a, weight_in).astype(bf)
    part_back = dot32(got_g, weight_out, contract).astype(bf)
    pre_b = part_pre.astype(jnp.float32) + other_core(part_pre).astype(jnp.float32)
    back_h = part_back.astype(jnp.float32) + other_core(part_back).astype(jnp.float32)
    sigma = jax.nn.sigmoid(pre_b)
    grad_hidden = (back_h * sigma * (1.0 + pre_b * (1.0 - sigma))).astype(bf)
    out_b = dot32(grad_hidden, weight_in, contract).astype(bf).reshape(experts, rows, cols)
    back_b = exchange(out_b).reshape(-1, cols)

    over_rows = (((0,), (0,)), ((), ()))
    sum_f = dot32(mix_f, back_f, over_rows).astype(bf)
    sum_b = dot32(mix_b, back_b, over_rows).astype(bf)

    def settle(total, by):
        near = moved(total[:tok], by, False)
        far = moved(total[tok:], by, True)
        return (near.astype(jnp.float32) + far.astype(jnp.float32)).astype(bf)

    return settle(sum_f, 1), settle(sum_b, -1)


def solution(mesh):
    devices = mesh.devices
    sections, nodes, locals_ = devices.shape
    fine = Mesh(devices.reshape(sections, nodes, 2, 4, locals_ // 8), ("section", "node", "zhi", "x", "y"))
    where = ("zhi", "x", "y")
    tokens = P(("section",) + where, "node")
    picks = P(("section",) + where, None)
    in_specs = (
        tokens,
        picks,
        picks,
        tokens,
        tokens,
        picks,
        picks,
        P("section", where, "node", None),
        P("section", where, None, "node"),
    )
    return jax.shard_map(
        local, mesh=fine, in_specs=in_specs, out_specs=(tokens, tokens), check_vma=False
    )
```

```python
import jax
import jax.numpy as jnp
from jax import lax
from jax.sharding import Mesh, PartitionSpec as P

CAP = 25
NODE = "node"
PLANE = ("x", "y")
RING = ("section", "zhi", "x", "y")


def pairs_of(shape, move):
    sections, halves, xs, ys = shape
    pairs = []
    for s in range(sections):
        for h in range(halves):
            for x in range(xs):
                for y in range(ys):
                    s2, h2 = move(s, h)
                    src = ((s * halves + h) * xs + x) * ys + y
                    dst = ((s2 * halves + h2) * xs + x) * ys + y
                    pairs.append((src, dst))
    return pairs


def moved(v, by, cross):
    shape = tuple(lax.axis_size(a) for a in RING)
    sections = shape[0]
    return lax.ppermute(
        v, RING, pairs_of(shape, lambda s, h: ((s + by) % sections, 1 - h if cross else h))
    )


def other_core(v):
    return lax.ppermute(v, NODE, [(0, 1), (1, 0)])


def exchange(v):
    return lax.all_to_all(v, PLANE, split_axis=0, concat_axis=0, tiled=True)


def note_of(routes, gates):
    note = jnp.concatenate([routes.astype(jnp.bfloat16).T, gates.T], axis=0)
    return jnp.pad(note, ((0, 16 - note.shape[0]), (0, 0)))


def places(note, top, first, experts):
    tokens = note.shape[1]
    routes = note[:top].astype(jnp.int32)
    gates = note[top : 2 * top].astype(jnp.float32)
    labels = first + jnp.arange(experts, dtype=jnp.int32)
    match = routes[:, None, :] == labels[None, :, None]
    chosen = jnp.sum(match.astype(jnp.float32), axis=0)
    weight = jnp.sum(jnp.where(match, gates[:, None, :], 0.0), axis=0)
    at = jnp.arange(tokens, dtype=jnp.int32)
    earlier = (at[:, None] < at[None, :]).astype(jnp.bfloat16)
    rank = jnp.dot(chosen.astype(jnp.bfloat16), earlier, preferred_element_type=jnp.float32)
    return jnp.where(chosen > 0, rank.astype(jnp.int32), -1), weight


def offset(place, by):
    return jnp.where(place >= 0, place + by, -1)


def hits(place, rows):
    return place[:, None, :] == jnp.arange(rows, dtype=jnp.int32)[None, :, None]


def pack(place, rows, tokens):
    experts = place.shape[0]
    send = hits(place, rows).astype(jnp.bfloat16).reshape(experts * rows, -1)
    return dot32(send, tokens).astype(jnp.bfloat16).reshape(experts, rows, -1)


def combine(place, weight, got):
    experts, rows, cols = got.shape
    mix = jnp.where(hits(place, rows), weight[:, None, :], 0.0).astype(jnp.bfloat16)
    over_rows = (((0,), (0,)), ((), ()))
    return dot32(mix.reshape(experts * rows, -1), got.reshape(-1, cols), over_rows).astype(
        jnp.bfloat16
    )


def after(value, *done):
    return lax.optimization_barrier((value,) + done)[0]


def dot32(a, b, dims=(((1,), (0,)), ((), ()))):
    return lax.dot_general(a, b, dims, preferred_element_type=jnp.float32)


def local(
    act_forward,
    routes_forward,
    gates_forward,
    act_backward,
    grad_backward,
    routes_backward,
    gates_backward,
    w_in,
    w_out,
):
    weight_in = w_in[0, 0]
    weight_out = w_out[0, 0]
    tok, cols = act_forward.shape
    top = routes_forward.shape[1]
    experts = lax.axis_size("x") * lax.axis_size("y")
    first = lax.axis_index("zhi") * experts
    bf = jnp.bfloat16
    contract = (((1,), (1,)), ((), ()))

    note_f = note_of(routes_forward, gates_forward)
    note_b = note_of(routes_backward, gates_backward)
    notes = jnp.concatenate([note_b, note_f], axis=1)
    both = jnp.concatenate([act_backward, grad_backward], axis=1)
    notes_wide = jnp.pad(notes, ((0, 0), (0, 2 * cols - notes.shape[1])))
    far_b = moved(jnp.concatenate([both, notes_wide], axis=0), 0, True)
    far_f = moved(after(act_forward, far_b), 0, True)

    place_f, weight_f = places(note_f, top, first, experts)
    place_b, weight_b = places(note_b, top, first, experts)
    own_rows = jnp.concatenate([act_forward, act_backward, grad_backward], axis=0)
    own_places = jnp.concatenate(
        [place_f, offset(place_b, CAP), offset(place_b, 2 * CAP)], axis=1
    )
    got_own = exchange(pack(own_places, (3 * CAP + 7) // 8 * 8, own_rows))

    far_place_b, far_weight_b = places(far_b[tok:, :tok], top, first, experts)
    far_place_f, far_weight_f = places(far_b[tok:, tok : 2 * tok], top, first, experts)
    padded = (CAP + 7) // 8 * 8
    got_far_b = exchange(after(pack(far_place_b, padded, far_b[:tok]), got_own))
    got_far_f = exchange(after(pack(far_place_f, padded, far_f), got_far_b))

    def added(part):
        part = part.astype(bf)
        return part.astype(jnp.float32) + other_core(part).astype(jnp.float32)

    def forward(pre):
        return dot32(jax.nn.silu(pre).astype(bf), weight_out).astype(bf)

    def backward(pre, back_h):
        sigma = jax.nn.sigmoid(pre)
        slope = (back_h * sigma * (1.0 + pre * (1.0 - sigma))).astype(bf)
        return dot32(slope, weight_in, contract).astype(bf)

    cut = experts * CAP
    own_fa = jnp.concatenate([got_own[:, :CAP], got_own[:, CAP : 2 * CAP]], axis=0)
    own_pre = added(dot32(own_fa.reshape(-1, cols), weight_in))
    own_back = added(
        dot32(got_own[:, 2 * CAP : 3 * CAP].reshape(-1, cols), weight_out, contract)
    )
    own_out_f = forward(own_pre[:cut]).reshape(experts, CAP, cols)
    own_out_b = backward(own_pre[cut:], own_back).reshape(experts, CAP, cols)

    rows_b = got_far_b.reshape(-1, 2 * cols)
    far_pre = added(dot32(rows_b[:, :cols], weight_in))
    far_back = added(dot32(rows_b[:, cols:], weight_out, contract))
    far_out_b = backward(far_pre, far_back).reshape(experts, padded, cols)
    far_out_f = forward(added(dot32(got_far_f.reshape(-1, cols), weight_in))).reshape(
        experts, padded, cols
    )

    def returned(far, own, *done):
        joined = jnp.concatenate([far[:, :CAP], own], axis=1)
        joined = jnp.pad(joined, ((0, 0), (0, (2 * CAP + 7) // 8 * 8 - 2 * CAP), (0, 0)))
        return exchange(after(joined, *done))

    back_b = returned(far_out_b, own_out_b, got_far_f)
    back_f = returned(far_out_f, own_out_f, back_b)

    def settle(back, far_place, far_weight, place, weight, by):
        both_places = jnp.concatenate([far_place, offset(place, CAP)], axis=1)
        total = combine(both_places, jnp.concatenate([far_weight, weight], axis=1), back)
        far = moved(total[:tok], by, True)
        near = moved(total[tok:], by, False)
        return (near.astype(jnp.float32) + far.astype(jnp.float32)).astype(bf)

    return (
        settle(back_f, far_place_f, far_weight_f, place_f, weight_f, 1),
        settle(back_b, far_place_b, far_weight_b, place_b, weight_b, -1),
    )


def solution(mesh):
    devices = mesh.devices
    sections, nodes, locals_ = devices.shape
    fine = Mesh(devices.reshape(sections, nodes, 2, 4, locals_ // 8), ("section", "node", "zhi", "x", "y"))
    where = ("zhi", "x", "y")
    tokens = P(("section",) + where, "node")
    picks = P(("section",) + where, None)
    in_specs = (
        tokens,
        picks,
        picks,
        tokens,
        tokens,
        picks,
        picks,
        P("section", where, "node", None),
        P("section", where, None, "node"),
    )
    return jax.shard_map(
        local, mesh=fine, in_specs=in_specs, out_specs=(tokens, tokens), check_vma=False
    )
```

```python
import jax
import jax.numpy as jnp
from jax import lax
from jax.sharding import Mesh, PartitionSpec as P

CAP = 25
NODE = "node"
PLANE = ("x", "y")
RING = ("section", "zhi", "x", "y")


def pairs_of(shape, move):
    sections, halves, xs, ys = shape
    pairs = []
    for s in range(sections):
        for h in range(halves):
            for x in range(xs):
                for y in range(ys):
                    s2, h2 = move(s, h)
                    src = ((s * halves + h) * xs + x) * ys + y
                    dst = ((s2 * halves + h2) * xs + x) * ys + y
                    pairs.append((src, dst))
    return pairs


def moved(v, by, cross):
    shape = tuple(lax.axis_size(a) for a in RING)
    sections = shape[0]
    return lax.ppermute(
        v, RING, pairs_of(shape, lambda s, h: ((s + by) % sections, 1 - h if cross else h))
    )


def other_core(v):
    return lax.ppermute(v, NODE, [(0, 1), (1, 0)])


def exchange(v):
    return lax.all_to_all(v, PLANE, split_axis=0, concat_axis=0, tiled=True)


def note_of(routes, gates):
    note = jnp.concatenate([routes.astype(jnp.bfloat16).T, gates.T], axis=0)
    return jnp.pad(note, ((0, 16 - note.shape[0]), (0, 0)))


def places(note, top, first, experts):
    tokens = note.shape[1]
    routes = note[:top].astype(jnp.int32)
    gates = note[top : 2 * top].astype(jnp.float32)
    labels = first + jnp.arange(experts, dtype=jnp.int32)
    match = routes[:, None, :] == labels[None, :, None]
    chosen = jnp.sum(match.astype(jnp.float32), axis=0)
    weight = jnp.sum(jnp.where(match, gates[:, None, :], 0.0), axis=0)
    at = jnp.arange(tokens, dtype=jnp.int32)
    earlier = (at[:, None] < at[None, :]).astype(jnp.bfloat16)
    rank = jnp.dot(chosen.astype(jnp.bfloat16), earlier, preferred_element_type=jnp.float32)
    return jnp.where(chosen > 0, rank.astype(jnp.int32), -1), weight


def offset(place, by):
    return jnp.where(place >= 0, place + by, -1)


def hits(place, rows):
    return place[:, None, :] == jnp.arange(rows, dtype=jnp.int32)[None, :, None]


def pack(place, rows, tokens):
    experts = place.shape[0]
    send = hits(place, rows).astype(jnp.bfloat16).reshape(experts * rows, -1)
    return dot32(send, tokens).astype(jnp.bfloat16).reshape(experts, rows, -1)


def combine(place, weight, got):
    experts, rows, cols = got.shape
    mix = jnp.where(hits(place, rows), weight[:, None, :], 0.0).astype(jnp.bfloat16)
    over_rows = (((0,), (0,)), ((), ()))
    return dot32(mix.reshape(experts * rows, -1), got.reshape(-1, cols), over_rows).astype(
        jnp.bfloat16
    )


def after(value, *done):
    return lax.optimization_barrier((value,) + done)[0]


def dot32(a, b, dims=(((1,), (0,)), ((), ()))):
    return lax.dot_general(a, b, dims, preferred_element_type=jnp.float32)


def local(
    act_forward,
    routes_forward,
    gates_forward,
    act_backward,
    grad_backward,
    routes_backward,
    gates_backward,
    w_in,
    w_out,
):
    weight_in = w_in[0, 0]
    weight_out = w_out[0, 0]
    tok, cols = act_forward.shape
    top = routes_forward.shape[1]
    experts = lax.axis_size("x") * lax.axis_size("y")
    first = lax.axis_index("zhi") * experts
    bf = jnp.bfloat16
    contract = (((1,), (1,)), ((), ()))

    eight = lambda n: (n + 7) // 8 * 8
    rows_in, rows_out = eight(3 * CAP), eight(2 * CAP)

    notes = jnp.concatenate(
        [note_of(routes_forward, gates_forward), note_of(routes_backward, gates_backward)], axis=1
    )
    notes = jnp.pad(notes, ((0, 0), (0, cols - notes.shape[1])))
    near = jnp.concatenate([act_forward, act_backward, grad_backward, notes], axis=0)
    far = moved(near, 0, True)

    def tables(block):
        note = block[3 * tok :]
        place_f, weight_f = places(note[:, :tok], top, first, experts)
        place_b, weight_b = places(note[:, tok : 2 * tok], top, first, experts)
        place_b1, place_b2 = offset(place_b, CAP), offset(place_b, 2 * CAP)
        into = jnp.concatenate([place_f, place_b1, place_b2], axis=1)
        back = jnp.concatenate([place_f, place_b1], axis=1)
        return into, back, jnp.concatenate([weight_f, weight_b], axis=1)

    def added(part):
        part = part.astype(bf)
        return part.astype(jnp.float32) + other_core(part).astype(jnp.float32)

    def work(got):
        rows = [got[:, i * CAP : (i + 1) * CAP].reshape(-1, cols) for i in range(3)]
        pre_f = added(dot32(rows[0], weight_in))
        pre_b = added(dot32(rows[1], weight_in))
        back_h = added(dot32(rows[2], weight_out, contract))
        out_f = dot32(jax.nn.silu(pre_f).astype(bf), weight_out).astype(bf)
        sigma = jax.nn.sigmoid(pre_b)
        slope = (back_h * sigma * (1.0 + pre_b * (1.0 - sigma))).astype(bf)
        out_b = dot32(slope, weight_in, contract).astype(bf)
        shape = (experts, CAP, cols)
        joined = jnp.concatenate([out_f.reshape(shape), out_b.reshape(shape)], axis=1)
        return jnp.pad(joined, ((0, 0), (0, rows_out - 2 * CAP), (0, 0)))

    into, back, weight = tables(near)
    got = exchange(pack(into, rows_in, near[: 3 * tok]))
    far = after(far, got)
    far_into, far_back, far_weight = tables(far)
    far_got = exchange(pack(far_into, rows_in, far[: 3 * tok]))
    out = work(got)
    far_out = exchange(work(far_got))
    far_sum = combine(far_back, far_weight, far_out)
    far_f = moved(far_sum[:tok], 1, True)
    far_b = moved(far_sum[tok:], -1, True)
    near_sum = combine(back, weight, exchange(after(out, far_out)))
    near_f = moved(near_sum[:tok], 1, False)
    near_b = moved(near_sum[tok:], -1, False)

    def both(a, b):
        return (a.astype(jnp.float32) + b.astype(jnp.float32)).astype(bf)

    return both(near_f, far_f), both(near_b, far_b)


def solution(mesh):
    devices = mesh.devices
    sections, nodes, locals_ = devices.shape
    fine = Mesh(devices.reshape(sections, nodes, 2, 4, locals_ // 8), ("section", "node", "zhi", "x", "y"))
    where = ("zhi", "x", "y")
    tokens = P(("section",) + where, "node")
    picks = P(("section",) + where, None)
    in_specs = (
        tokens,
        picks,
        picks,
        tokens,
        tokens,
        picks,
        picks,
        P("section", where, "node", None),
        P("section", where, None, "node"),
    )
    return jax.shard_map(
        local, mesh=fine, in_specs=in_specs, out_specs=(tokens, tokens), check_vma=False
    )
```

```python
import functools

import jax
import jax.numpy as jnp
from jax import lax
from jax.experimental import pallas as pl
from jax.experimental.pallas import tpu as pltpu
from jax.sharding import Mesh, PartitionSpec as P

SLOTS = 32
NODE = "node"
PLANE = ("x", "y")
RING = ("section", "zhi", "x", "y")
BF = jnp.bfloat16
F32 = jnp.float32
MATMUL = (((1,), (0,)), ((), ()))
TRANSPOSED = (((1,), (1,)), ((), ()))
OVER_ROWS = (((0,), (0,)), ((), ()))
WIDTH = 256


def pairs_of(shape, move):
    sections, halves, xs, ys = shape
    pairs = []
    for s in range(sections):
        for h in range(halves):
            for x in range(xs):
                for y in range(ys):
                    s2, h2 = move(s, h)
                    src = ((s * halves + h) * xs + x) * ys + y
                    dst = ((s2 * halves + h2) * xs + x) * ys + y
                    pairs.append((src, dst))
    return pairs


def moved(v, by, cross):
    shape = tuple(lax.axis_size(a) for a in RING)
    sections = shape[0]
    return lax.ppermute(
        v, RING, pairs_of(shape, lambda s, h: ((s + by) % sections, 1 - h if cross else h))
    )


def other_core(v):
    return lax.ppermute(v, NODE, [(0, 1), (1, 0)])


def exchange(v):
    return lax.all_to_all(v, PLANE, split_axis=0, concat_axis=0, tiled=True)


def after(value, *done):
    return lax.optimization_barrier((value,) + done)[0]


def dot32(a, b, dims=MATMUL):
    return lax.dot_general(a, b, dims, preferred_element_type=F32)


def run(kernel, outs, *args, scalars=0):
    where = [pl.BlockSpec(memory_space=pltpu.SMEM)] * scalars
    where += [pl.BlockSpec(memory_space=pltpu.VMEM)] * (len(args) - scalars)
    return pl.pallas_call(
        kernel,
        out_shape=outs,
        in_specs=where,
        out_specs=jax.tree.map(lambda _: pl.BlockSpec(memory_space=pltpu.VMEM), outs),
        compiler_params=pltpu.CompilerParams(vmem_limit_bytes=32 << 20),
        cost_estimate=pl.CostEstimate(flops=1000, bytes_accessed=1000, transcendentals=0),
    )(*args)


def shaped(*shape):
    return jax.ShapeDtypeStruct(shape, BF)


def note_of(routes, gates):
    note = jnp.concatenate([routes.astype(BF).T, gates.T], axis=0)
    return jnp.pad(note, ((0, 16 - note.shape[0]), (0, 0)))


def tables(note, first, top, experts):
    tokens = note.shape[1] // 2
    label = (lax.broadcasted_iota(jnp.int32, (experts, 2 * tokens), 0) + first).astype(F32)
    chosen = jnp.zeros((experts, 2 * tokens), F32)
    weight = jnp.zeros((experts, 2 * tokens), F32)
    for k in range(top):
        match = note[k : k + 1] == label
        chosen = chosen + jnp.where(match, 1.0, 0.0)
        weight = weight + jnp.where(match, note[top + k : top + k + 1], 0.0)
    i = lax.broadcasted_iota(jnp.int32, (tokens, tokens), 0)
    j = lax.broadcasted_iota(jnp.int32, (tokens, tokens), 1)
    earlier = jnp.where(i < j, 1.0, 0.0).astype(BF)
    slot = lax.broadcasted_iota(jnp.int32, (SLOTS, tokens), 0).astype(F32)
    result = []
    for half in range(2):
        span = slice(half * tokens, (half + 1) * tokens)
        rank = dot32(chosen[:, span].astype(BF), earlier)
        place = jnp.where(chosen[:, span] > 0.0, rank, -1.0)
        hit = [jnp.where(slot == place[e : e + 1], 1.0, 0.0) for e in range(experts)]
        mix = [hit[e] * weight[e : e + 1, span] for e in range(experts)]
        result.append(
            (jnp.concatenate(hit, axis=0).astype(BF), jnp.concatenate(mix, axis=0).astype(BF))
        )
    return result


def put(out_ref, at, hit, rows_ref, first=0):
    experts = out_ref.shape[0]
    tokens = hit.shape[1]
    for c in range(0, out_ref.shape[2], WIDTH):
        block = dot32(hit, rows_ref[first : first + tokens, c : c + WIDTH]).astype(BF)
        out_ref[:, at : at + SLOTS, c : c + WIDTH] = block.reshape(experts, SLOTS, WIDTH)


def pack_own(top, first_ref, f_ref, a_ref, g_ref, note_ref, out_ref, mix_f_ref, mix_b_ref):
    (hit_f, mix_f), (hit_b, mix_b) = tables(
        note_ref[...].astype(F32), first_ref[0], top, out_ref.shape[0]
    )
    mix_f_ref[...] = mix_f
    mix_b_ref[...] = mix_b
    put(out_ref, 0, hit_f, f_ref)
    put(out_ref, SLOTS, hit_b, a_ref)
    put(out_ref, 2 * SLOTS, hit_b, g_ref)


def pack_far(top, first_ref, far_ref, out_ref, hit_f_ref, mix_f_ref, mix_b_ref):
    tokens = hit_f_ref.shape[1]
    note = far_ref[2 * tokens :, : 2 * tokens].astype(F32)
    (hit_f, mix_f), (hit_b, mix_b) = tables(note, first_ref[0], top, out_ref.shape[0])
    hit_f_ref[...] = hit_f
    mix_f_ref[...] = mix_f
    mix_b_ref[...] = mix_b
    put(out_ref, 0, hit_b, far_ref)
    put(out_ref, SLOTS, hit_b, far_ref, tokens)


def pack_more(hit_ref, rows_ref, out_ref):
    put(out_ref, 0, hit_ref[...], rows_ref)


def parts(kinds, got_ref, w_in_ref, w_out_ref, out_ref):
    experts, _, cols = got_ref.shape
    hidden = w_in_ref.shape[1]
    rows = experts * SLOTS
    for i, kind in enumerate(kinds):
        x = got_ref[:, i * SLOTS : (i + 1) * SLOTS, :].reshape(rows, cols)
        for c in range(0, hidden, WIDTH):
            if kind == "g":
                part = dot32(x, w_out_ref[c : c + WIDTH, :], TRANSPOSED)
            else:
                part = dot32(x, w_in_ref[:, c : c + WIDTH])
            out_ref[i * rows : (i + 1) * rows, c : c + WIDTH] = part.astype(BF)


def results(kinds, mine_ref, theirs_ref, w_in_ref, w_out_ref, out_ref, hold_ref):
    experts, _, cols = out_ref.shape
    rows = experts * SLOTS
    hidden = w_in_ref.shape[1]

    def total(i, c):
        span = (slice(i * rows, (i + 1) * rows), slice(c, c + WIDTH))
        return mine_ref[span].astype(F32) + theirs_ref[span].astype(F32)

    i, at = 0, 0
    while i < len(kinds):
        forward = kinds[i] == "f"
        for c in range(0, hidden, WIDTH):
            pre = total(i, c)
            sigma = 1.0 / (1.0 + jnp.exp(-pre))
            if forward:
                value = pre * sigma
            else:
                value = total(i + 1, c) * sigma * (1.0 + pre * (1.0 - sigma))
            hold_ref[:, c : c + WIDTH] = value.astype(BF)
        for c in range(0, cols, WIDTH):
            if forward:
                block = dot32(hold_ref[...], w_out_ref[:, c : c + WIDTH])
            else:
                block = dot32(hold_ref[...], w_in_ref[c : c + WIDTH, :], TRANSPOSED)
            out_ref[:, at : at + SLOTS, c : c + WIDTH] = block.astype(BF).reshape(
                experts, SLOTS, WIDTH
            )
        i += 1 if forward else 2
        at += SLOTS


def sums(count, *refs):
    mixes, back_ref, outs = refs[:count], refs[count], refs[count + 1 :]
    experts, _, cols = back_ref.shape
    for i in range(count):
        mix = mixes[i][...]
        for c in range(0, cols, WIDTH):
            rows = back_ref[:, i * SLOTS : (i + 1) * SLOTS, c : c + WIDTH]
            rows = rows.reshape(experts * SLOTS, WIDTH)
            outs[i][:, c : c + WIDTH] = dot32(mix, rows, OVER_ROWS).astype(BF)


def local(
    act_forward,
    routes_forward,
    gates_forward,
    act_backward,
    grad_backward,
    routes_backward,
    gates_backward,
    w_in,
    w_out,
):
    weight_in = w_in[0, 0]
    weight_out = w_out[0, 0]
    tok, cols = act_forward.shape
    hidden = weight_in.shape[1]
    top = routes_forward.shape[1]
    experts = lax.axis_size("x") * lax.axis_size("y")
    rows = experts * SLOTS
    first = (lax.axis_index("zhi") * experts).astype(jnp.int32).reshape(1)
    table = shaped(rows, tok)

    note = jnp.concatenate(
        [note_of(routes_forward, gates_forward), note_of(routes_backward, gates_backward)], axis=1
    )
    wide = jnp.pad(note, ((0, 0), (0, cols - note.shape[1])))

    def work(got, kinds, many):
        mine = run(
            functools.partial(parts, kinds),
            shaped(len(kinds) * rows, hidden),
            got,
            weight_in,
            weight_out,
        )
        theirs = other_core(mine)
        return pl.pallas_call(
            functools.partial(results, kinds),
            out_shape=shaped(experts, many * SLOTS, cols),
            in_specs=[pl.BlockSpec(memory_space=pltpu.VMEM)] * 4,
            out_specs=pl.BlockSpec(memory_space=pltpu.VMEM),
            scratch_shapes=[pltpu.VMEM((rows, hidden), BF)],
            compiler_params=pltpu.CompilerParams(vmem_limit_bytes=32 << 20),
            cost_estimate=pl.CostEstimate(flops=1000, bytes_accessed=1000, transcendentals=0),
        )(mine, theirs, weight_in, weight_out)

    def combined(back, *mixes):
        return run(
            functools.partial(sums, len(mixes)), (shaped(tok, cols),) * len(mixes), *mixes, back
        )

    far_b = moved(jnp.concatenate([act_backward, grad_backward, wide], axis=0), 0, True)
    far_f = moved(after(act_forward, far_b), 0, True)

    sent, mix_f, mix_b = run(
        functools.partial(pack_own, top),
        (shaped(experts, 3 * SLOTS, cols), table, table),
        first,
        act_forward,
        act_backward,
        grad_backward,
        note,
        scalars=1,
    )
    got = exchange(sent)
    sent_b, far_hit_f, far_mix_f, far_mix_b = run(
        functools.partial(pack_far, top),
        (shaped(experts, 2 * SLOTS, cols), table, table, table),
        first,
        after(far_b, got),
        scalars=1,
    )
    got_b = exchange(sent_b)
    out = work(after(got, sent_b), "fag", 2)
    sent_f = run(pack_more, shaped(experts, SLOTS, cols), far_hit_f, after(far_f, out))
    got_f = exchange(after(sent_f, got_b))
    out_b = work(after(got_b, sent_f), "ag", 1)
    back_b = exchange(after(out_b, got_f))
    out_f = work(after(got_f, out_b), "f", 1)
    back_f = exchange(after(out_f, back_b))
    (far_sum_b,) = combined(back_b, far_mix_b)
    over_b = moved(far_sum_b, -1, True)
    (far_sum_f,) = combined(back_f, far_mix_f)
    over_f = moved(far_sum_f, 1, True)
    sum_f, sum_b = combined(exchange(after(out, far_sum_f)), mix_f, mix_b)
    near_f = moved(sum_f, 1, False)
    near_b = moved(sum_b, -1, False)

    def both(a, b):
        return (a.astype(F32) + b.astype(F32)).astype(BF)

    return both(near_f, over_f), both(near_b, over_b)


def solution(mesh):
    devices = mesh.devices
    sections, nodes, locals_ = devices.shape
    fine = Mesh(
        devices.reshape(sections, nodes, 2, 4, locals_ // 8), ("section", "node", "zhi", "x", "y")
    )
    where = ("zhi", "x", "y")
    tokens = P(("section",) + where, "node")
    picks = P(("section",) + where, None)
    in_specs = (
        tokens,
        picks,
        picks,
        tokens,
        tokens,
        picks,
        picks,
        P("section", where, "node", None),
        P("section", where, None, "node"),
    )
    return jax.shard_map(
        local, mesh=fine, in_specs=in_specs, out_specs=(tokens, tokens), check_vma=False
    )
```

```python
import functools

import jax
import jax.numpy as jnp
from jax import lax
from jax.experimental import pallas as pl
from jax.experimental.pallas import tpu as pltpu
from jax.sharding import Mesh, PartitionSpec as P

SLOTS = 32
NODE = "node"
PLANE = ("x", "y")
RING = ("section", "zhi", "x", "y")
BF = jnp.bfloat16
F32 = jnp.float32
MATMUL = (((1,), (0,)), ((), ()))
TRANSPOSED = (((1,), (1,)), ((), ()))
OVER_ROWS = (((0,), (0,)), ((), ()))
WIDTH = 256
LONG = 40_000_000_000


def pairs_of(shape, move):
    sections, halves, xs, ys = shape
    pairs = []
    for s in range(sections):
        for h in range(halves):
            for x in range(xs):
                for y in range(ys):
                    s2, h2 = move(s, h)
                    src = ((s * halves + h) * xs + x) * ys + y
                    dst = ((s2 * halves + h2) * xs + x) * ys + y
                    pairs.append((src, dst))
    return pairs


def moved(v, by, cross):
    shape = tuple(lax.axis_size(a) for a in RING)
    sections = shape[0]
    return lax.ppermute(
        v, RING, pairs_of(shape, lambda s, h: ((s + by) % sections, 1 - h if cross else h))
    )


def other_core(v):
    return lax.ppermute(v, NODE, [(0, 1), (1, 0)])


def in_pieces(v, count):
    each = v.shape[0] // count
    return jnp.concatenate([other_core(v[i * each : (i + 1) * each]) for i in range(count)], axis=0)


def exchange(v):
    return lax.all_to_all(v, PLANE, split_axis=0, concat_axis=0, tiled=True)


def after(value, *done):
    return lax.optimization_barrier((value,) + done)[0]


def dot32(a, b, dims=MATMUL):
    return lax.dot_general(a, b, dims, preferred_element_type=F32)


def run(kernel, outs, *args, scalars=0, scratch=(), flops=1000):
    where = [pl.BlockSpec(memory_space=pltpu.SMEM)] * scalars
    where += [pl.BlockSpec(memory_space=pltpu.VMEM)] * (len(args) - scalars)
    return pl.pallas_call(
        kernel,
        out_shape=outs,
        in_specs=where,
        out_specs=jax.tree.map(lambda _: pl.BlockSpec(memory_space=pltpu.VMEM), outs),
        scratch_shapes=scratch,
        compiler_params=pltpu.CompilerParams(vmem_limit_bytes=32 << 20),
        cost_estimate=pl.CostEstimate(flops=flops, bytes_accessed=1000, transcendentals=0),
    )(*args)


def shaped(*shape):
    return jax.ShapeDtypeStruct(shape, BF)


def gather_block(a_ref, g_ref, *refs):
    notes, out_ref, hold_ref = refs[:4], refs[4], refs[5]
    tokens = a_ref.shape[0]
    top = notes[0].shape[0]
    out_ref[:tokens, :] = a_ref[...]
    out_ref[tokens : 2 * tokens, :] = g_ref[...]
    hold_ref[...] = jnp.zeros(hold_ref.shape, F32)
    for half in range(2):
        span = slice(half * tokens, (half + 1) * tokens)
        hold_ref[:top, span] = notes[2 * half][...].astype(F32)
        hold_ref[8 : 8 + top, span] = notes[2 * half + 1][...].astype(F32)
    out_ref[2 * tokens :, :] = hold_ref[...].astype(BF)


def tables(note, first, top, experts):
    tokens = note.shape[1] // 2
    label = (lax.broadcasted_iota(jnp.int32, (experts, 2 * tokens), 0) + first).astype(F32)
    chosen = jnp.zeros((experts, 2 * tokens), F32)
    weight = jnp.zeros((experts, 2 * tokens), F32)
    for k in range(top):
        match = note[k : k + 1] == label
        chosen = chosen + jnp.where(match, 1.0, 0.0)
        weight = weight + jnp.where(match, note[8 + k : 9 + k], 0.0)
    i = lax.broadcasted_iota(jnp.int32, (tokens, tokens), 0)
    j = lax.broadcasted_iota(jnp.int32, (tokens, tokens), 1)
    earlier = jnp.where(i < j, 1.0, 0.0).astype(BF)
    slot = lax.broadcasted_iota(jnp.int32, (SLOTS, tokens), 0).astype(F32)
    result = []
    for half in range(2):
        span = slice(half * tokens, (half + 1) * tokens)
        rank = dot32(chosen[:, span].astype(BF), earlier)
        place = jnp.where(chosen[:, span] > 0.0, rank, -1.0)
        hit = [jnp.where(slot == place[e : e + 1], 1.0, 0.0) for e in range(experts)]
        mix = [hit[e] * weight[e : e + 1, span] for e in range(experts)]
        result.append(
            (jnp.concatenate(hit, axis=0).astype(BF), jnp.concatenate(mix, axis=0).astype(BF))
        )
    return result


def put(out_ref, at, hit, rows_ref, first=0):
    experts = out_ref.shape[0]
    tokens = hit.shape[1]
    for c in range(0, out_ref.shape[2], WIDTH):
        block = dot32(hit, rows_ref[first : first + tokens, c : c + WIDTH]).astype(BF)
        out_ref[:, at : at + SLOTS, c : c + WIDTH] = block.reshape(experts, SLOTS, WIDTH)


def pack_first(top, near, *refs):
    if near:
        first_ref, block_ref, f_ref, out_ref, mix_f_ref, mix_b_ref = refs
    else:
        first_ref, block_ref, out_ref, mix_f_ref, mix_b_ref, hit_f_ref = refs
    tokens = mix_f_ref.shape[1]
    note = block_ref[2 * tokens :, : 2 * tokens].astype(F32)
    (hit_f, mix_f), (hit_b, mix_b) = tables(note, first_ref[0], top, out_ref.shape[0])
    mix_f_ref[...] = mix_f
    mix_b_ref[...] = mix_b
    put(out_ref, 0, hit_b, block_ref)
    put(out_ref, SLOTS, hit_b, block_ref, tokens)
    if near:
        put(out_ref, 2 * SLOTS, hit_f, f_ref)
    else:
        hit_f_ref[...] = hit_f


def pack_more(hit_ref, rows_ref, out_ref):
    put(out_ref, 0, hit_ref[...], rows_ref)


def parts(kinds, got_ref, w_in_ref, w_out_ref, out_ref):
    experts, _, cols = got_ref.shape
    hidden = w_in_ref.shape[1]
    rows = experts * SLOTS
    for i, kind in enumerate(kinds):
        x = got_ref[:, i * SLOTS : (i + 1) * SLOTS, :].reshape(rows, cols)
        for c in range(0, hidden, WIDTH):
            if kind == "g":
                part = dot32(x, w_out_ref[c : c + WIDTH, :], TRANSPOSED)
            else:
                part = dot32(x, w_in_ref[:, c : c + WIDTH])
            out_ref[i * rows : (i + 1) * rows, c : c + WIDTH] = part.astype(BF)


def results(kinds, held, mine_ref, theirs_ref, w_in_ref, w_out_ref, *refs):
    out_ref, hold_ref = refs[-2:]
    experts, _, cols = out_ref.shape
    rows = experts * SLOTS
    hidden = w_in_ref.shape[1]

    def total(i, c):
        span = (slice(i * rows, (i + 1) * rows), slice(c, c + WIDTH))
        return mine_ref[span].astype(F32) + theirs_ref[span].astype(F32)

    i, at = 0, 0
    if held:
        at = refs[0].shape[1]
        out_ref[:, :at, :] = refs[0][...]
    while i < len(kinds):
        forward = kinds[i] == "f"
        for c in range(0, hidden, WIDTH):
            pre = total(i, c)
            sigma = 1.0 / (1.0 + jnp.exp(-pre))
            if forward:
                value = pre * sigma
            else:
                value = total(i + 1, c) * sigma * (1.0 + pre * (1.0 - sigma))
            hold_ref[:, c : c + WIDTH] = value.astype(BF)
        for c in range(0, cols, WIDTH):
            if forward:
                block = dot32(hold_ref[...], w_out_ref[:, c : c + WIDTH])
            else:
                block = dot32(hold_ref[...], w_in_ref[c : c + WIDTH, :], TRANSPOSED)
            out_ref[:, at : at + SLOTS, c : c + WIDTH] = block.astype(BF).reshape(
                experts, SLOTS, WIDTH
            )
        i += 1 if forward else 2
        at += SLOTS


def sums(count, *refs):
    mixes, back_ref, outs = refs[:count], refs[count], refs[count + 1 :]
    experts, _, cols = back_ref.shape
    for i in range(count):
        mix = mixes[i][...]
        for c in range(0, cols, WIDTH):
            rows = back_ref[:, i * SLOTS : (i + 1) * SLOTS, c : c + WIDTH]
            rows = rows.reshape(experts * SLOTS, WIDTH)
            outs[i][:, c : c + WIDTH] = dot32(mix, rows, OVER_ROWS).astype(BF)


def hold(a_ref, b_ref, x_ref, y_ref):
    x_ref[...] = a_ref[...]
    y_ref[...] = b_ref[...]


def add(a_ref, b_ref, c_ref, d_ref, x_ref, y_ref):
    x_ref[...] = (a_ref[...].astype(F32) + c_ref[...].astype(F32)).astype(BF)
    y_ref[...] = (b_ref[...].astype(F32) + d_ref[...].astype(F32)).astype(BF)


def local(
    act_forward,
    routes_forward,
    gates_forward,
    act_backward,
    grad_backward,
    routes_backward,
    gates_backward,
    w_in,
    w_out,
):
    weight_in = w_in[0, 0]
    weight_out = w_out[0, 0]
    tok, cols = act_forward.shape
    hidden = weight_in.shape[1]
    top = routes_forward.shape[1]
    experts = lax.axis_size("x") * lax.axis_size("y")
    rows = experts * SLOTS
    first = (lax.axis_index("zhi") * experts).astype(jnp.int32).reshape(1)
    table = shaped(rows, tok)

    def work(got, kinds, *held):
        mine = run(
            functools.partial(parts, kinds),
            shaped(len(kinds) * rows, hidden),
            got,
            weight_in,
            weight_out,
        )
        theirs = other_core(mine) if len(kinds) < 2 else in_pieces(mine, len(kinds))
        many = kinds.count("f") + kinds.count("a") + len(held)
        return run(
            functools.partial(results, kinds, len(held)),
            shaped(experts, many * SLOTS, cols),
            mine,
            theirs,
            weight_in,
            weight_out,
            *held,
            scratch=[pltpu.VMEM((rows, hidden), BF)],
        )

    def combined(back, *mixes):
        return run(
            functools.partial(sums, len(mixes)), (shaped(tok, cols),) * len(mixes), *mixes, back
        )

    block = run(
        gather_block,
        shaped(2 * tok + 16, cols),
        act_backward,
        grad_backward,
        routes_forward.T,
        gates_forward.T,
        routes_backward.T,
        gates_backward.T,
        scratch=[pltpu.VMEM((16, cols), F32)],
    )
    far_block = moved(block, 0, True)
    far_rows = moved(after(act_forward, far_block), 0, True)

    sent, mix_f, mix_b = run(
        functools.partial(pack_first, top, True),
        (shaped(experts, 3 * SLOTS, cols), table, table),
        first,
        block,
        act_forward,
        scalars=1,
    )
    got = exchange(sent)
    sent_b, far_mix_f, far_mix_b, far_hit_f = run(
        functools.partial(pack_first, top, False),
        (shaped(experts, 2 * SLOTS, cols), table, table, table),
        first,
        far_block,
        scalars=1,
        flops=LONG,
    )
    got_b = exchange(after(sent_b, got))
    sent_f = run(pack_more, shaped(experts, SLOTS, cols), far_hit_f, far_rows, flops=LONG)
    got_f = exchange(after(sent_f, got_b))
    out_b = work(after(got_b, sent_f), "ag")
    out_bf = work(after(got_f, out_b), "f", out_b)
    far_out = exchange(out_bf)
    out = work(after(got, out_bf), "agf")
    far_sum_b, far_sum_f = combined(after(far_out, out), far_mix_b, far_mix_f)
    over = (moved(far_sum_b, -1, True), moved(far_sum_f, 1, True))
    back = exchange(after(out, far_sum_f))
    sum_b, sum_f = combined(back, mix_b, mix_f)
    near = (moved(sum_b, -1, False), moved(sum_f, 1, False))
    pair = (shaped(tok, cols),) * 2
    over = run(hold, pair, *over, flops=LONG)
    input_grad, layer_out = run(add, pair, *near, *over)
    return layer_out, input_grad


def solution(mesh):
    devices = mesh.devices
    sections, nodes, locals_ = devices.shape
    fine = Mesh(
        devices.reshape(sections, nodes, 2, 4, locals_ // 8), ("section", "node", "zhi", "x", "y")
    )
    where = ("zhi", "x", "y")
    tokens = P(("section",) + where, "node")
    picks = P(("section",) + where, None)
    in_specs = (
        tokens,
        picks,
        picks,
        tokens,
        tokens,
        picks,
        picks,
        P("section", where, "node", None),
        P("section", where, None, "node"),
    )
    return jax.shard_map(
        local, mesh=fine, in_specs=in_specs, out_specs=(tokens, tokens), check_vma=False
    )
```

```python
import functools

import jax
import jax.numpy as jnp
from jax import lax
from jax.experimental import pallas as pl
from jax.experimental.pallas import tpu as pltpu
from jax.sharding import Mesh, PartitionSpec as P

SLOTS = 32
NODE = "node"
PLANE = ("x", "y")
RING = ("section", "zhi", "x", "y")
BF = jnp.bfloat16
F32 = jnp.float32
MATMUL = (((1,), (0,)), ((), ()))
TRANSPOSED = (((1,), (1,)), ((), ()))
OVER_ROWS = (((0,), (0,)), ((), ()))
WIDTH = 256
LONG = 40_000_000_000


def pairs_of(shape, move):
    sections, halves, xs, ys = shape
    pairs = []
    for s in range(sections):
        for h in range(halves):
            for x in range(xs):
                for y in range(ys):
                    s2, h2 = move(s, h)
                    src = ((s * halves + h) * xs + x) * ys + y
                    dst = ((s2 * halves + h2) * xs + x) * ys + y
                    pairs.append((src, dst))
    return pairs


def moved(v, by, cross):
    shape = tuple(lax.axis_size(a) for a in RING)
    sections = shape[0]
    return lax.ppermute(
        v, RING, pairs_of(shape, lambda s, h: ((s + by) % sections, 1 - h if cross else h))
    )


def other_core(v):
    return lax.ppermute(v, NODE, [(0, 1), (1, 0)])


def exchange(v):
    return lax.all_to_all(v, PLANE, split_axis=0, concat_axis=0, tiled=True)


def after(value, *done):
    return lax.optimization_barrier((value,) + done)[0]


def dot32(a, b, dims=MATMUL):
    return lax.dot_general(a, b, dims, preferred_element_type=F32)


def run(kernel, outs, *args, scalars=0, scratch=(), flops=1000, room=32 << 20):
    where = [pl.BlockSpec(memory_space=pltpu.SMEM)] * scalars
    where += [pl.BlockSpec(memory_space=pltpu.VMEM)] * (len(args) - scalars)
    return pl.pallas_call(
        kernel,
        out_shape=outs,
        in_specs=where,
        out_specs=jax.tree.map(lambda _: pl.BlockSpec(memory_space=pltpu.VMEM), outs),
        scratch_shapes=scratch,
        compiler_params=pltpu.CompilerParams(vmem_limit_bytes=room),
        cost_estimate=pl.CostEstimate(flops=flops, bytes_accessed=1000, transcendentals=0),
    )(*args)


def shaped(*shape):
    return jax.ShapeDtypeStruct(shape, BF)


def gather_block(f_ref, *refs):
    notes, out_ref, hold_ref = refs[:4], refs[4], refs[5]
    tokens = f_ref.shape[0]
    top = notes[0].shape[0]
    out_ref[:tokens, :] = f_ref[...]
    hold_ref[...] = jnp.zeros(hold_ref.shape, F32)
    for half in range(2):
        span = slice(half * tokens, (half + 1) * tokens)
        hold_ref[:top, span] = notes[2 * half][...].astype(F32)
        hold_ref[8 : 8 + top, span] = notes[2 * half + 1][...].astype(F32)
    out_ref[tokens:, :] = hold_ref[...].astype(BF)


def tables(note, first, top, experts):
    tokens = note.shape[1] // 2
    label = (lax.broadcasted_iota(jnp.int32, (experts, 2 * tokens), 0) + first).astype(F32)
    chosen = jnp.zeros((experts, 2 * tokens), F32)
    weight = jnp.zeros((experts, 2 * tokens), F32)
    for k in range(top):
        match = note[k : k + 1] == label
        chosen = chosen + jnp.where(match, 1.0, 0.0)
        weight = weight + jnp.where(match, note[8 + k : 9 + k], 0.0)
    i = lax.broadcasted_iota(jnp.int32, (tokens, tokens), 0)
    j = lax.broadcasted_iota(jnp.int32, (tokens, tokens), 1)
    earlier = jnp.where(i < j, 1.0, 0.0).astype(BF)
    slot = lax.broadcasted_iota(jnp.int32, (SLOTS, tokens), 0).astype(F32)
    result = []
    for half in range(2):
        span = slice(half * tokens, (half + 1) * tokens)
        rank = dot32(chosen[:, span].astype(BF), earlier)
        place = jnp.where(chosen[:, span] > 0.0, rank, -1.0)
        hit = [jnp.where(slot == place[e : e + 1], 1.0, 0.0) for e in range(experts)]
        mix = [hit[e] * weight[e : e + 1, span] for e in range(experts)]
        result.append(
            (jnp.concatenate(hit, axis=0).astype(BF), jnp.concatenate(mix, axis=0).astype(BF))
        )
    return result


def put(out_ref, at, hit, rows_ref):
    experts = out_ref.shape[0]
    tokens = hit.shape[1]
    for c in range(0, out_ref.shape[2], WIDTH):
        block = dot32(hit, rows_ref[:tokens, c : c + WIDTH]).astype(BF)
        out_ref[:, at : at + SLOTS, c : c + WIDTH] = block.reshape(experts, SLOTS, WIDTH)


def block_tables(top, first_ref, block_ref, experts, tokens):
    note = block_ref[tokens:, : 2 * tokens].astype(F32)
    return tables(note, first_ref[0], top, experts)


def pack_near(top, first_ref, block_ref, a_ref, g_ref, out_ref, mix_f_ref, mix_b_ref):
    (hit_f, mix_f), (hit_b, mix_b) = block_tables(
        top, first_ref, block_ref, out_ref.shape[0], a_ref.shape[0]
    )
    mix_f_ref[...] = mix_f
    mix_b_ref[...] = mix_b
    put(out_ref, 0, hit_b, a_ref)
    put(out_ref, SLOTS, hit_b, g_ref)
    put(out_ref, 2 * SLOTS, hit_f, block_ref)


def pack_far_f(top, first_ref, block_ref, out_ref, mix_f_ref, mix_b_ref, hit_b_ref):
    (hit_f, mix_f), (hit_b, mix_b) = block_tables(
        top, first_ref, block_ref, out_ref.shape[0], mix_f_ref.shape[1]
    )
    mix_f_ref[...] = mix_f
    mix_b_ref[...] = mix_b
    hit_b_ref[...] = hit_b
    put(out_ref, 0, hit_f, block_ref)


def pack_far_b(hit_ref, a_ref, g_ref, out_ref):
    put(out_ref, 0, hit_ref[...], a_ref)
    put(out_ref, SLOTS, hit_ref[...], g_ref)


def parts(kinds, got_ref, w_in_ref, w_out_ref, *outs):
    experts, _, cols = got_ref.shape
    for i, kind in enumerate(kinds):
        x = got_ref[:, i * SLOTS : (i + 1) * SLOTS, :].reshape(experts * SLOTS, cols)
        for c in range(0, w_in_ref.shape[1], WIDTH):
            if kind == "g":
                part = dot32(x, w_out_ref[c : c + WIDTH, :], TRANSPOSED)
            else:
                part = dot32(x, w_in_ref[:, c : c + WIDTH])
            outs[i][:, c : c + WIDTH] = part.astype(BF)


def results(kinds, *refs):
    mine, theirs = refs[: len(kinds)], refs[len(kinds) : 2 * len(kinds)]
    w_in_ref, w_out_ref, out_ref, hold_ref = refs[2 * len(kinds) :]
    experts, _, cols = out_ref.shape
    hidden = w_in_ref.shape[1]

    def total(i, c):
        span = slice(c, c + WIDTH)
        return mine[i][:, span].astype(F32) + theirs[i][:, span].astype(F32)

    i, at = 0, 0
    while i < len(kinds):
        forward = kinds[i] == "f"
        for c in range(0, hidden, WIDTH):
            pre = total(i, c)
            sigma = 1.0 / (1.0 + jnp.exp(-pre))
            if forward:
                value = pre * sigma
            else:
                value = total(i + 1, c) * sigma * (1.0 + pre * (1.0 - sigma))
            hold_ref[:, c : c + WIDTH] = value.astype(BF)
        for c in range(0, cols, WIDTH):
            if forward:
                block = dot32(hold_ref[...], w_out_ref[:, c : c + WIDTH])
            else:
                block = dot32(hold_ref[...], w_in_ref[c : c + WIDTH, :], TRANSPOSED)
            out_ref[:, at : at + SLOTS, c : c + WIDTH] = block.astype(BF).reshape(
                experts, SLOTS, WIDTH
            )
        i += 1 if forward else 2
        at += SLOTS


def sums(count, *refs):
    mixes, backs, outs = refs[:count], refs[count:-count], refs[-count:]
    experts, _, cols = backs[0].shape
    for i in range(count):
        mix = mixes[i][...]
        back_ref, at = (backs[i], 0) if len(backs) > 1 else (backs[0], i * SLOTS)
        for c in range(0, cols, WIDTH):
            rows = back_ref[:, at : at + SLOTS, c : c + WIDTH]
            rows = rows.reshape(experts * SLOTS, WIDTH)
            outs[i][:, c : c + WIDTH] = dot32(mix, rows, OVER_ROWS).astype(BF)


def hold(a_ref, b_ref, x_ref, y_ref):
    x_ref[...] = a_ref[...]
    y_ref[...] = b_ref[...]


def add(a_ref, b_ref, c_ref, d_ref, x_ref, y_ref):
    x_ref[...] = (a_ref[...].astype(F32) + c_ref[...].astype(F32)).astype(BF)
    y_ref[...] = (b_ref[...].astype(F32) + d_ref[...].astype(F32)).astype(BF)


def local(
    act_forward,
    routes_forward,
    gates_forward,
    act_backward,
    grad_backward,
    routes_backward,
    gates_backward,
    w_in,
    w_out,
):
    weight_in = w_in[0, 0]
    weight_out = w_out[0, 0]
    tok, cols = act_forward.shape
    hidden = weight_in.shape[1]
    top = routes_forward.shape[1]
    experts = lax.axis_size("x") * lax.axis_size("y")
    rows = experts * SLOTS
    first = (lax.axis_index("zhi") * experts).astype(jnp.int32).reshape(1)
    table = shaped(rows, tok)

    def work(got, kinds):
        mine = run(
            functools.partial(parts, kinds),
            (shaped(rows, hidden),) * len(kinds),
            got,
            weight_in,
            weight_out,
        )
        theirs = [other_core(part) for part in mine]
        many = kinds.count("f") + kinds.count("a")
        return run(
            functools.partial(results, kinds),
            shaped(experts, many * SLOTS, cols),
            *mine,
            *theirs,
            weight_in,
            weight_out,
            scratch=[pltpu.VMEM((rows, hidden), BF)],
        )

    def combined(back, *mixes):
        return run(
            functools.partial(sums, len(mixes)), (shaped(tok, cols),) * len(mixes), *mixes, *back
        )

    block = run(
        gather_block,
        shaped(tok + 16, cols),
        act_forward,
        routes_forward.T,
        gates_forward.T,
        routes_backward.T,
        gates_backward.T,
        scratch=[pltpu.VMEM((16, cols), F32)],
        room=56 << 20,
    )
    far_block = moved(block, 0, True)
    far_a = moved(after(act_backward, far_block), 0, True)
    far_g = moved(after(grad_backward, far_block), 0, True)

    sent, mix_f, mix_b = run(
        functools.partial(pack_near, top),
        (shaped(experts, 3 * SLOTS, cols), table, table),
        first,
        block,
        act_backward,
        grad_backward,
        scalars=1,
        room=56 << 20,
    )
    got = exchange(sent)
    sent_f, far_mix_f, far_mix_b, far_hit_b = run(
        functools.partial(pack_far_f, top),
        (shaped(experts, SLOTS, cols), table, table, table),
        first,
        far_block,
        scalars=1,
        flops=LONG,
    )
    got_f = exchange(after(sent_f, got))
    sent_b = run(
        pack_far_b, shaped(experts, 2 * SLOTS, cols), far_hit_b, far_a, far_g, flops=LONG
    )
    got_b = exchange(after(sent_b, got_f))
    out = work(after(got, sent_b, got_f), "agf")
    out_f = work(after(got_f, out), "f")
    back_f = exchange(after(out_f, got_b))
    out_b = work(after(got_b, out_f), "ag")
    back_b = exchange(after(out_b, back_f))
    far_sum_b, far_sum_f = combined((back_b, back_f), far_mix_b, far_mix_f)
    over = (moved(far_sum_b, -1, True), moved(far_sum_f, 1, True))
    back = exchange(after(out, far_sum_f))
    sum_b, sum_f = combined((back,), mix_b, mix_f)
    near = (moved(sum_b, -1, False), moved(sum_f, 1, False))
    pair = (shaped(tok, cols),) * 2
    over = run(hold, pair, *over, flops=LONG)
    input_grad, layer_out = run(add, pair, *near, *over)
    return layer_out, input_grad


def solution(mesh):
    devices = mesh.devices
    sections, nodes, locals_ = devices.shape
    fine = Mesh(
        devices.reshape(sections, nodes, 2, 4, locals_ // 8), ("section", "node", "zhi", "x", "y")
    )
    where = ("zhi", "x", "y")
    tokens = P(("section",) + where, "node")
    picks = P(("section",) + where, None)
    in_specs = (
        tokens,
        picks,
        picks,
        tokens,
        tokens,
        picks,
        picks,
        P("section", where, "node", None),
        P("section", where, None, "node"),
    )
    return jax.shard_map(
        local, mesh=fine, in_specs=in_specs, out_specs=(tokens, tokens), check_vma=False
    )
```

```python
import functools

import jax
import jax.numpy as jnp
from jax import lax
from jax.experimental import pallas as pl
from jax.experimental.pallas import tpu as pltpu
from jax.sharding import Mesh, PartitionSpec as P

SLOTS = 32
HEAD = 24
LANES = 128
NODE = "node"
PLANE = ("x", "y")
RING = ("section", "zhi", "x", "y")
BF = jnp.bfloat16
F32 = jnp.float32
MATMUL = (((1,), (0,)), ((), ()))
TRANSPOSED = (((1,), (1,)), ((), ()))
OVER_ROWS = (((0,), (0,)), ((), ()))
WIDTH = 256
LONG = 40_000_000_000


def pairs_of(shape, move):
    sections, halves, xs, ys = shape
    pairs = []
    for s in range(sections):
        for h in range(halves):
            for x in range(xs):
                for y in range(ys):
                    s2, h2 = move(s, h)
                    src = ((s * halves + h) * xs + x) * ys + y
                    dst = ((s2 * halves + h2) * xs + x) * ys + y
                    pairs.append((src, dst))
    return pairs


def moved(v, by, cross):
    shape = tuple(lax.axis_size(a) for a in RING)
    sections = shape[0]
    return lax.ppermute(
        v, RING, pairs_of(shape, lambda s, h: ((s + by) % sections, 1 - h if cross else h))
    )


def other_core(v):
    return lax.ppermute(v, NODE, [(0, 1), (1, 0)])


def exchange(v):
    return lax.all_to_all(v, PLANE, split_axis=0, concat_axis=0, tiled=True)


def after(value, *done):
    return lax.optimization_barrier((value,) + done)[0]


def dot32(a, b, dims=MATMUL):
    return lax.dot_general(a, b, dims, preferred_element_type=F32)


def run(kernel, outs, *args, scalars=0, scratch=(), flops=1000, room=32 << 20):
    where = [pl.BlockSpec(memory_space=pltpu.SMEM)] * scalars
    where += [pl.BlockSpec(memory_space=pltpu.VMEM)] * (len(args) - scalars)
    return pl.pallas_call(
        kernel,
        out_shape=outs,
        in_specs=where,
        out_specs=jax.tree.map(lambda _: pl.BlockSpec(memory_space=pltpu.VMEM), outs),
        scratch_shapes=scratch,
        compiler_params=pltpu.CompilerParams(vmem_limit_bytes=room),
        cost_estimate=pl.CostEstimate(flops=flops, bytes_accessed=1000, transcendentals=0),
    )(*args)


def shaped(*shape):
    return jax.ShapeDtypeStruct(shape, BF)


def gather_block(f_ref, *refs):
    notes, out_ref, hold_ref = refs[:4], refs[4], refs[5]
    tokens = f_ref.shape[0]
    top = notes[0].shape[0]
    out_ref[:tokens, :] = f_ref[...]
    hold_ref[...] = jnp.zeros(hold_ref.shape, F32)
    for half in range(2):
        span = slice(half * tokens, (half + 1) * tokens)
        hold_ref[:top, span] = notes[2 * half][...].astype(F32)
        hold_ref[8 : 8 + top, span] = notes[2 * half + 1][...].astype(F32)
    out_ref[tokens:, :] = hold_ref[...].astype(BF)


def tables(note, first, top, experts):
    tokens = note.shape[1] // 2
    label = (lax.broadcasted_iota(jnp.int32, (experts, 2 * tokens), 0) + first).astype(F32)
    chosen = jnp.zeros((experts, 2 * tokens), F32)
    weight = jnp.zeros((experts, 2 * tokens), F32)
    for k in range(top):
        match = note[k : k + 1] == label
        chosen = chosen + jnp.where(match, 1.0, 0.0)
        weight = weight + jnp.where(match, note[8 + k : 9 + k], 0.0)
    i = lax.broadcasted_iota(jnp.int32, (tokens, tokens), 0)
    j = lax.broadcasted_iota(jnp.int32, (tokens, tokens), 1)
    earlier = jnp.where(i < j, 1.0, 0.0).astype(BF)
    slot = lax.broadcasted_iota(jnp.int32, (SLOTS, tokens), 0).astype(F32)
    result = []
    for half in range(2):
        span = slice(half * tokens, (half + 1) * tokens)
        rank = dot32(chosen[:, span].astype(BF), earlier)
        place = jnp.where(chosen[:, span] > 0.0, rank, -1.0)
        hit = [jnp.where(slot == place[e : e + 1], 1.0, 0.0) for e in range(experts)]
        mix = [hit[e] * weight[e : e + 1, span] for e in range(experts)]
        result.append(
            (jnp.concatenate(hit, axis=0).astype(BF), jnp.concatenate(mix, axis=0).astype(BF))
        )
    return result


def flat(x):
    blocks = x.shape[1] // LANES
    pieces = [x[:HEAD, c * LANES : (c + 1) * LANES] for c in range(blocks)]
    at = lax.broadcasted_iota(jnp.int32, (blocks, LANES), 0)
    last = jnp.zeros((blocks, LANES), F32)
    for c in range(blocks):
        row = x[HEAD : HEAD + 1, c * LANES : (c + 1) * LANES]
        last = jnp.where(at == c, jnp.broadcast_to(row, (blocks, LANES)), last)
    return jnp.concatenate(pieces + [last], axis=0)


def unflat(y):
    blocks = y.shape[0] // (HEAD + 1)
    tail = SLOTS - HEAD
    columns = []
    for c in range(blocks):
        row = y[blocks * HEAD + c : blocks * HEAD + c + 1]
        column = [y[c * HEAD : (c + 1) * HEAD], jnp.broadcast_to(row, (tail, LANES))]
        columns.append(jnp.concatenate(column, axis=0))
    return jnp.concatenate(columns, axis=1)


def ship(out_ref, wides):
    for e in range(out_ref.shape[0]):
        rows = [flat(wide[e * SLOTS : (e + 1) * SLOTS, :]) for wide in wides]
        out_ref[e] = jnp.concatenate(rows, axis=0).astype(BF)


def unship(got_ref, wides):
    each = got_ref.shape[1] // len(wides)
    for e in range(got_ref.shape[0]):
        rows = got_ref[e].astype(F32)
        for i, wide in enumerate(wides):
            wide[e * SLOTS : (e + 1) * SLOTS, :] = unflat(rows[i * each : (i + 1) * each]).astype(BF)


def put(wide_ref, hit, rows_ref):
    tokens = hit.shape[1]
    for c in range(0, wide_ref.shape[1], WIDTH):
        wide_ref[:, c : c + WIDTH] = dot32(hit, rows_ref[:tokens, c : c + WIDTH])


def block_tables(top, first_ref, block_ref, experts, tokens):
    note = block_ref[tokens:, : 2 * tokens].astype(F32)
    return tables(note, first_ref[0], top, experts)


def pack_near(top, first_ref, block_ref, a_ref, g_ref, out_ref, mix_f_ref, mix_b_ref, *wides):
    (hit_f, mix_f), (hit_b, mix_b) = block_tables(
        top, first_ref, block_ref, out_ref.shape[0], a_ref.shape[0]
    )
    mix_f_ref[...] = mix_f
    mix_b_ref[...] = mix_b
    put(wides[0], hit_b, a_ref)
    put(wides[1], hit_b, g_ref)
    put(wides[2], hit_f, block_ref)
    ship(out_ref, wides)


def pack_far_f(top, first_ref, block_ref, out_ref, mix_f_ref, mix_b_ref, hit_b_ref, *wides):
    (hit_f, mix_f), (hit_b, mix_b) = block_tables(
        top, first_ref, block_ref, out_ref.shape[0], mix_f_ref.shape[1]
    )
    mix_f_ref[...] = mix_f
    mix_b_ref[...] = mix_b
    hit_b_ref[...] = hit_b
    put(wides[0], hit_f, block_ref)
    ship(out_ref, wides)


def pack_far_b(hit_ref, a_ref, g_ref, out_ref, *wides):
    put(wides[0], hit_ref[...], a_ref)
    put(wides[1], hit_ref[...], g_ref)
    ship(out_ref, wides)


def parts(groups, *refs):
    kinds = "".join(groups)
    gots, refs = refs[: len(groups)], refs[len(groups) :]
    w_in_ref, w_out_ref, *refs = refs
    outs, wides = refs[: len(kinds)], refs[len(kinds) :]
    at = 0
    for got_ref, group in zip(gots, groups):
        unship(got_ref, wides[at : at + len(group)])
        at += len(group)
    for kind, wide, out_ref in zip(kinds, wides, outs):
        for c in range(0, w_in_ref.shape[1], WIDTH):
            if kind == "g":
                part = dot32(wide[...], w_out_ref[c : c + WIDTH, :], TRANSPOSED)
            else:
                part = dot32(wide[...], w_in_ref[:, c : c + WIDTH])
            out_ref[:, c : c + WIDTH] = part.astype(BF)


def results(groups, *refs):
    kinds = "".join(groups)
    mine, theirs = refs[: len(kinds)], refs[len(kinds) : 2 * len(kinds)]
    w_in_ref, w_out_ref, *refs = refs[2 * len(kinds) :]
    outs, hold_ref, wides = refs[: len(groups)], refs[len(groups)], refs[len(groups) + 1 :]
    hidden, cols = w_in_ref.shape[1], w_in_ref.shape[0]

    def total(i, c):
        span = slice(c, c + WIDTH)
        return mine[i][:, span].astype(F32) + theirs[i][:, span].astype(F32)

    i = 0
    for wide in wides:
        forward = kinds[i] == "f"
        for c in range(0, hidden, WIDTH):
            pre = total(i, c)
            sigma = 1.0 / (1.0 + jnp.exp(-pre))
            if forward:
                value = pre * sigma
            else:
                value = total(i + 1, c) * sigma * (1.0 + pre * (1.0 - sigma))
            hold_ref[:, c : c + WIDTH] = value.astype(BF)
        for c in range(0, cols, WIDTH):
            if forward:
                block = dot32(hold_ref[...], w_out_ref[:, c : c + WIDTH])
            else:
                block = dot32(hold_ref[...], w_in_ref[c : c + WIDTH, :], TRANSPOSED)
            wide[:, c : c + WIDTH] = block
        i += 1 if forward else 2
    at = 0
    for out_ref, group in zip(outs, groups):
        many = made(group)
        ship(out_ref, wides[at : at + many])
        at += many


def made(group):
    return group.count("f") + group.count("a")


def sums(count, *refs):
    mixes, wides = refs[:count], refs[-count:]
    backs, outs = refs[count : -2 * count], refs[-2 * count : -count]
    for i, back_ref in enumerate(backs):
        unship(back_ref, [wides[i]] if len(backs) > 1 else wides)
    for mix_ref, wide, out_ref in zip(mixes, wides, outs):
        for c in range(0, out_ref.shape[1], WIDTH):
            total = dot32(mix_ref[...], wide[:, c : c + WIDTH], OVER_ROWS)
            out_ref[:, c : c + WIDTH] = total.astype(BF)


def hold(a_ref, b_ref, x_ref, y_ref):
    x_ref[...] = a_ref[...]
    y_ref[...] = b_ref[...]


def add(a_ref, b_ref, c_ref, d_ref, x_ref, y_ref):
    x_ref[...] = (a_ref[...].astype(F32) + c_ref[...].astype(F32)).astype(BF)
    y_ref[...] = (b_ref[...].astype(F32) + d_ref[...].astype(F32)).astype(BF)


def local(
    act_forward,
    routes_forward,
    gates_forward,
    act_backward,
    grad_backward,
    routes_backward,
    gates_backward,
    w_in,
    w_out,
):
    weight_in = w_in[0, 0]
    weight_out = w_out[0, 0]
    tok, cols = act_forward.shape
    hidden = weight_in.shape[1]
    top = routes_forward.shape[1]
    experts = lax.axis_size("x") * lax.axis_size("y")
    rows = experts * SLOTS
    first = (lax.axis_index("zhi") * experts).astype(jnp.int32).reshape(1)
    table = shaped(rows, tok)

    def wide(count, dtype):
        return [pltpu.VMEM((rows, cols), dtype)] * count

    def sendable(kinds):
        return shaped(experts, kinds * (HEAD + 1) * (cols // LANES), LANES)

    def work(gots, *groups):
        count = len("".join(groups))
        mine = run(
            functools.partial(parts, groups),
            (shaped(rows, hidden),) * count,
            *gots,
            weight_in,
            weight_out,
            scratch=wide(count, BF),
        )
        theirs = [other_core(part) for part in mine]
        return run(
            functools.partial(results, groups),
            tuple(sendable(made(group)) for group in groups),
            *mine,
            *theirs,
            weight_in,
            weight_out,
            scratch=[pltpu.VMEM((rows, hidden), BF)] + wide(made("".join(groups)), F32),
        )

    def combined(back, *mixes):
        return run(
            functools.partial(sums, len(mixes)),
            (shaped(tok, cols),) * len(mixes),
            *mixes,
            *back,
            scratch=wide(len(mixes), BF),
        )

    block = run(
        gather_block,
        shaped(tok + 16, cols),
        act_forward,
        routes_forward.T,
        gates_forward.T,
        routes_backward.T,
        gates_backward.T,
        scratch=[pltpu.VMEM((16, cols), F32)],
        room=56 << 20,
    )
    far_block = moved(block, 0, True)
    far_a = moved(after(act_backward, far_block), 0, True)
    far_g = moved(after(grad_backward, far_block), 0, True)

    sent, mix_f, mix_b = run(
        functools.partial(pack_near, top),
        (sendable(3), table, table),
        first,
        block,
        act_backward,
        grad_backward,
        scalars=1,
        scratch=wide(3, F32),
        room=56 << 20,
    )
    got = exchange(sent)
    sent_f, far_mix_f, far_mix_b, far_hit_b = run(
        functools.partial(pack_far_f, top),
        (sendable(1), table, table, table),
        first,
        far_block,
        scalars=1,
        scratch=wide(1, F32),
        flops=LONG,
    )
    got_f = exchange(after(sent_f, got))
    sent_b = run(
        pack_far_b,
        sendable(2),
        far_hit_b,
        far_a,
        far_g,
        scratch=wide(2, F32),
        flops=LONG,
    )
    got_b = exchange(after(sent_b, got_f))
    out, out_f = work((after(got, sent_b), got_f), "agf", "f")
    back_f = exchange(after(out_f, got_b))
    (out_b,) = work((after(got_b, out_f),), "ag")
    back_b = exchange(after(out_b, back_f))
    far_sum_b, far_sum_f = combined((back_b, back_f), far_mix_b, far_mix_f)
    over = (moved(far_sum_b, -1, True), moved(far_sum_f, 1, True))
    back = exchange(after(out, far_sum_f))
    sum_b, sum_f = combined((back,), mix_b, mix_f)
    near = (moved(sum_b, -1, False), moved(sum_f, 1, False))
    pair = (shaped(tok, cols),) * 2
    over = run(hold, pair, *over, flops=LONG)
    input_grad, layer_out = run(add, pair, *near, *over)
    return layer_out, input_grad


def solution(mesh):
    devices = mesh.devices
    sections, nodes, locals_ = devices.shape
    fine = Mesh(
        devices.reshape(sections, nodes, 2, 4, locals_ // 8), ("section", "node", "zhi", "x", "y")
    )
    where = ("zhi", "x", "y")
    tokens = P(("section",) + where, "node")
    picks = P(("section",) + where, None)
    in_specs = (
        tokens,
        picks,
        picks,
        tokens,
        tokens,
        picks,
        picks,
        P("section", where, "node", None),
        P("section", where, None, "node"),
    )
    return jax.shard_map(
        local, mesh=fine, in_specs=in_specs, out_specs=(tokens, tokens), check_vma=False
    )
```

```python
import functools

import jax
import jax.numpy as jnp
from jax import lax
from jax.experimental import pallas as pl
from jax.experimental.pallas import tpu as pltpu
from jax.sharding import Mesh, PartitionSpec as P

SLOTS = 32
HEAD = 24
LANES = 128
NODE = "node"
PLANE = ("x", "y")
RING = ("section", "zhi", "x", "y")
BF = jnp.bfloat16
F32 = jnp.float32
MATMUL = (((1,), (0,)), ((), ()))
TRANSPOSED = (((1,), (1,)), ((), ()))
OVER_ROWS = (((0,), (0,)), ((), ()))
WIDTH = 256
LONG = 40_000_000_000


def pairs_of(shape, move):
    sections, halves, xs, ys = shape
    pairs = []
    for s in range(sections):
        for h in range(halves):
            for x in range(xs):
                for y in range(ys):
                    s2, h2 = move(s, h)
                    src = ((s * halves + h) * xs + x) * ys + y
                    dst = ((s2 * halves + h2) * xs + x) * ys + y
                    pairs.append((src, dst))
    return pairs


def moved(v, by, cross):
    shape = tuple(lax.axis_size(a) for a in RING)
    sections = shape[0]
    return lax.ppermute(
        v, RING, pairs_of(shape, lambda s, h: ((s + by) % sections, 1 - h if cross else h))
    )


def other_core(v):
    return lax.ppermute(v, NODE, [(0, 1), (1, 0)])


def exchange(v):
    return lax.all_to_all(v, PLANE, split_axis=0, concat_axis=0, tiled=True)


def after(value, *done):
    return lax.optimization_barrier((value,) + done)[0]


def dot32(a, b, dims=MATMUL):
    return lax.dot_general(a, b, dims, preferred_element_type=F32)


def run(kernel, outs, *args, scalars=0, scratch=(), flops=1000, room=32 << 20):
    where = [pl.BlockSpec(memory_space=pltpu.SMEM)] * scalars
    where += [pl.BlockSpec(memory_space=pltpu.VMEM)] * (len(args) - scalars)
    return pl.pallas_call(
        kernel,
        out_shape=outs,
        in_specs=where,
        out_specs=jax.tree.map(lambda _: pl.BlockSpec(memory_space=pltpu.VMEM), outs),
        scratch_shapes=scratch,
        compiler_params=pltpu.CompilerParams(vmem_limit_bytes=room),
        cost_estimate=pl.CostEstimate(flops=flops, bytes_accessed=1000, transcendentals=0),
    )(*args)


def shaped(*shape):
    return jax.ShapeDtypeStruct(shape, BF)


def gather_block(a_ref, g_ref, *refs):
    notes, out_ref, hold_ref = refs[:4], refs[4], refs[5]
    tokens = a_ref.shape[0]
    top = notes[0].shape[0]
    out_ref[:tokens, :] = a_ref[...]
    out_ref[tokens : 2 * tokens, :] = g_ref[...]
    hold_ref[...] = jnp.zeros(hold_ref.shape, F32)
    for half in range(2):
        span = slice(half * tokens, (half + 1) * tokens)
        hold_ref[:top, span] = notes[2 * half][...].astype(F32)
        hold_ref[8 : 8 + top, span] = notes[2 * half + 1][...].astype(F32)
    out_ref[2 * tokens :, :] = hold_ref[...].astype(BF)


def tables(note, first, top, experts):
    tokens = note.shape[1] // 2
    label = (lax.broadcasted_iota(jnp.int32, (experts, 2 * tokens), 0) + first).astype(F32)
    chosen = jnp.zeros((experts, 2 * tokens), F32)
    weight = jnp.zeros((experts, 2 * tokens), F32)
    for k in range(top):
        match = note[k : k + 1] == label
        chosen = chosen + jnp.where(match, 1.0, 0.0)
        weight = weight + jnp.where(match, note[8 + k : 9 + k], 0.0)
    i = lax.broadcasted_iota(jnp.int32, (tokens, tokens), 0)
    j = lax.broadcasted_iota(jnp.int32, (tokens, tokens), 1)
    earlier = jnp.where(i < j, 1.0, 0.0).astype(BF)
    slot = lax.broadcasted_iota(jnp.int32, (SLOTS, tokens), 0).astype(F32)
    result = []
    for half in range(2):
        span = slice(half * tokens, (half + 1) * tokens)
        rank = dot32(chosen[:, span].astype(BF), earlier)
        place = jnp.where(chosen[:, span] > 0.0, rank, -1.0)
        hit = [jnp.where(slot == place[e : e + 1], 1.0, 0.0) for e in range(experts)]
        mix = [hit[e] * weight[e : e + 1, span] for e in range(experts)]
        result.append(
            (jnp.concatenate(hit, axis=0).astype(BF), jnp.concatenate(mix, axis=0).astype(BF))
        )
    return result


def flat(x):
    blocks = x.shape[1] // LANES
    pieces = [x[:HEAD, c * LANES : (c + 1) * LANES] for c in range(blocks)]
    at = lax.broadcasted_iota(jnp.int32, (blocks, LANES), 0)
    last = jnp.zeros((blocks, LANES), F32)
    for c in range(blocks):
        row = x[HEAD : HEAD + 1, c * LANES : (c + 1) * LANES]
        last = jnp.where(at == c, jnp.broadcast_to(row, (blocks, LANES)), last)
    return jnp.concatenate(pieces + [last], axis=0)


def unflat(y):
    blocks = y.shape[0] // (HEAD + 1)
    tail = SLOTS - HEAD
    columns = []
    for c in range(blocks):
        row = y[blocks * HEAD + c : blocks * HEAD + c + 1]
        column = [y[c * HEAD : (c + 1) * HEAD], jnp.broadcast_to(row, (tail, LANES))]
        columns.append(jnp.concatenate(column, axis=0))
    return jnp.concatenate(columns, axis=1)


def ship(out_ref, wides):
    for e in range(out_ref.shape[0]):
        rows = [flat(wide[e * SLOTS : (e + 1) * SLOTS, :]) for wide in wides]
        out_ref[e] = jnp.concatenate(rows, axis=0).astype(BF)


def unship(got_ref, wides):
    each = got_ref.shape[1] // len(wides)
    for e in range(got_ref.shape[0]):
        rows = got_ref[e].astype(F32)
        for i, wide in enumerate(wides):
            wide[e * SLOTS : (e + 1) * SLOTS, :] = unflat(rows[i * each : (i + 1) * each]).astype(BF)


def put(wide_ref, hit, rows_ref, first=0):
    rows = slice(first, first + hit.shape[1])
    for c in range(0, wide_ref.shape[1], WIDTH):
        wide_ref[:, c : c + WIDTH] = dot32(hit, rows_ref[rows, c : c + WIDTH])


def block_tables(top, first_ref, block_ref, experts, tokens):
    note = block_ref[2 * tokens :, : 2 * tokens].astype(F32)
    return tables(note, first_ref[0], top, experts)


def pack_near(top, first_ref, block_ref, f_ref, out_ref, mix_f_ref, mix_b_ref, *wides):
    tokens = f_ref.shape[0]
    (hit_f, mix_f), (hit_b, mix_b) = block_tables(
        top, first_ref, block_ref, out_ref.shape[0], tokens
    )
    mix_f_ref[...] = mix_f
    mix_b_ref[...] = mix_b
    put(wides[0], hit_b, block_ref)
    put(wides[1], hit_b, block_ref, tokens)
    put(wides[2], hit_f, f_ref)
    ship(out_ref, wides)


def pack_far_b(top, first_ref, block_ref, out_ref, mix_f_ref, mix_b_ref, hit_f_ref, *wides):
    tokens = mix_f_ref.shape[1]
    (hit_f, mix_f), (hit_b, mix_b) = block_tables(
        top, first_ref, block_ref, out_ref.shape[0], tokens
    )
    mix_f_ref[...] = mix_f
    mix_b_ref[...] = mix_b
    hit_f_ref[...] = hit_f
    put(wides[0], hit_b, block_ref)
    put(wides[1], hit_b, block_ref, tokens)
    ship(out_ref, wides)


def pack_far_f(hit_ref, f_ref, out_ref, *wides):
    put(wides[0], hit_ref[...], f_ref)
    ship(out_ref, wides)


def parts(groups, *refs):
    kinds = "".join(groups)
    gots, refs = refs[: len(groups)], refs[len(groups) :]
    w_in_ref, w_out_ref, *refs = refs
    outs, wides = refs[: len(kinds)], refs[len(kinds) :]
    at = 0
    for got_ref, group in zip(gots, groups):
        unship(got_ref, wides[at : at + len(group)])
        at += len(group)
    for kind, wide, out_ref in zip(kinds, wides, outs):
        for c in range(0, w_in_ref.shape[1], WIDTH):
            if kind == "g":
                part = dot32(wide[...], w_out_ref[c : c + WIDTH, :], TRANSPOSED)
            else:
                part = dot32(wide[...], w_in_ref[:, c : c + WIDTH])
            out_ref[:, c : c + WIDTH] = part.astype(BF)


def results(groups, *refs):
    kinds = "".join(groups)
    mine, theirs = refs[: len(kinds)], refs[len(kinds) : 2 * len(kinds)]
    w_in_ref, w_out_ref, *refs = refs[2 * len(kinds) :]
    outs, hold_ref, wides = refs[: len(groups)], refs[len(groups)], refs[len(groups) + 1 :]
    hidden, cols = w_in_ref.shape[1], w_in_ref.shape[0]

    def total(i, c):
        span = slice(c, c + WIDTH)
        return mine[i][:, span].astype(F32) + theirs[i][:, span].astype(F32)

    i = 0
    for wide in wides:
        forward = kinds[i] == "f"
        for c in range(0, hidden, WIDTH):
            pre = total(i, c)
            sigma = 1.0 / (1.0 + jnp.exp(-pre))
            if forward:
                value = pre * sigma
            else:
                value = total(i + 1, c) * sigma * (1.0 + pre * (1.0 - sigma))
            hold_ref[:, c : c + WIDTH] = value.astype(BF)
        for c in range(0, cols, WIDTH):
            if forward:
                block = dot32(hold_ref[...], w_out_ref[:, c : c + WIDTH])
            else:
                block = dot32(hold_ref[...], w_in_ref[c : c + WIDTH, :], TRANSPOSED)
            wide[:, c : c + WIDTH] = block
        i += 1 if forward else 2
    at = 0
    for out_ref, group in zip(outs, groups):
        many = made(group)
        ship(out_ref, wides[at : at + many])
        at += many


def made(group):
    return group.count("f") + group.count("a")


def sums(count, *refs):
    mixes, wides = refs[:count], refs[-count:]
    backs, outs = refs[count : -2 * count], refs[-2 * count : -count]
    for i, back_ref in enumerate(backs):
        unship(back_ref, [wides[i]] if len(backs) > 1 else wides)
    for mix_ref, wide, out_ref in zip(mixes, wides, outs):
        for c in range(0, out_ref.shape[1], WIDTH):
            total = dot32(mix_ref[...], wide[:, c : c + WIDTH], OVER_ROWS)
            out_ref[:, c : c + WIDTH] = total.astype(BF)


def hold(a_ref, b_ref, x_ref, y_ref):
    x_ref[...] = a_ref[...]
    y_ref[...] = b_ref[...]


def add(a_ref, b_ref, c_ref, d_ref, x_ref, y_ref):
    x_ref[...] = (a_ref[...].astype(F32) + c_ref[...].astype(F32)).astype(BF)
    y_ref[...] = (b_ref[...].astype(F32) + d_ref[...].astype(F32)).astype(BF)


def local(
    act_forward,
    routes_forward,
    gates_forward,
    act_backward,
    grad_backward,
    routes_backward,
    gates_backward,
    w_in,
    w_out,
):
    weight_in = w_in[0, 0]
    weight_out = w_out[0, 0]
    tok, cols = act_forward.shape
    hidden = weight_in.shape[1]
    top = routes_forward.shape[1]
    experts = lax.axis_size("x") * lax.axis_size("y")
    rows = experts * SLOTS
    first = (lax.axis_index("zhi") * experts).astype(jnp.int32).reshape(1)
    table = shaped(rows, tok)

    def wide(count, dtype):
        return [pltpu.VMEM((rows, cols), dtype)] * count

    def sendable(kinds):
        return shaped(experts, kinds * (HEAD + 1) * (cols // LANES), LANES)

    def work(gots, *groups):
        count = len("".join(groups))
        mine = run(
            functools.partial(parts, groups),
            (shaped(rows, hidden),) * count,
            *gots,
            weight_in,
            weight_out,
            scratch=wide(count, BF),
        )
        theirs = [other_core(part) for part in mine]
        return run(
            functools.partial(results, groups),
            tuple(sendable(made(group)) for group in groups),
            *mine,
            *theirs,
            weight_in,
            weight_out,
            scratch=[pltpu.VMEM((rows, hidden), BF)] + wide(made("".join(groups)), F32),
        )

    def combined(back, *mixes):
        return run(
            functools.partial(sums, len(mixes)),
            (shaped(tok, cols),) * len(mixes),
            *mixes,
            *back,
            scratch=wide(len(mixes), BF),
        )

    block = run(
        gather_block,
        shaped(2 * tok + 16, cols),
        act_backward,
        grad_backward,
        routes_forward.T,
        gates_forward.T,
        routes_backward.T,
        gates_backward.T,
        scratch=[pltpu.VMEM((16, cols), F32)],
        room=56 << 20,
    )
    far_block = moved(block, 0, True)
    far_rows = moved(after(act_forward, far_block), 0, True)

    sent, mix_f, mix_b = run(
        functools.partial(pack_near, top),
        (sendable(3), table, table),
        first,
        block,
        act_forward,
        scalars=1,
        scratch=wide(3, F32),
        room=56 << 20,
    )
    got = exchange(sent)
    sent_b, far_mix_f, far_mix_b, far_hit_f = run(
        functools.partial(pack_far_b, top),
        (sendable(2), table, table, table),
        first,
        far_block,
        scalars=1,
        scratch=wide(2, F32),
        flops=LONG,
    )
    got_b = exchange(after(sent_b, got))
    sent_f = run(pack_far_f, sendable(1), far_hit_f, far_rows, scratch=wide(1, F32), flops=LONG)
    got_f = exchange(after(sent_f, got_b))
    (out_b,) = work((after(got_b, sent_f),), "ag")
    back_b = exchange(after(out_b, got_f))
    (out_f,) = work((after(got_f, out_b),), "f")
    back_f = exchange(after(out_f, back_b))
    (out,) = work((after(got, out_f),), "agf")
    back_f = after(back_f, out)
    far_sum_b, far_sum_f = combined((back_b, back_f), far_mix_b, far_mix_f)
    over = (moved(far_sum_b, -1, True), moved(far_sum_f, 1, True))
    back = exchange(after(out, far_sum_f))
    sum_b, sum_f = combined((back,), mix_b, mix_f)
    near = (moved(sum_b, -1, False), moved(sum_f, 1, False))
    pair = (shaped(tok, cols),) * 2
    over = run(hold, pair, *over, flops=LONG)
    input_grad, layer_out = run(add, pair, *near, *over)
    return layer_out, input_grad


def solution(mesh):
    devices = mesh.devices
    sections, nodes, locals_ = devices.shape
    fine = Mesh(
        devices.reshape(sections, nodes, 2, 4, locals_ // 8), ("section", "node", "zhi", "x", "y")
    )
    where = ("zhi", "x", "y")
    tokens = P(("section",) + where, "node")
    picks = P(("section",) + where, None)
    in_specs = (
        tokens,
        picks,
        picks,
        tokens,
        tokens,
        picks,
        picks,
        P("section", where, "node", None),
        P("section", where, None, "node"),
    )
    return jax.shard_map(
        local, mesh=fine, in_specs=in_specs, out_specs=(tokens, tokens), check_vma=False
    )
```

```python
import functools

import jax
import jax.numpy as jnp
from jax import lax
from jax.experimental import pallas as pl
from jax.experimental.pallas import tpu as pltpu
from jax.sharding import Mesh, PartitionSpec as P

SLOTS = 32
HEAD = 24
LANES = 128
NODE = "node"
PLANE = ("x", "y")
RING = ("section", "zhi", "x", "y")
BF = jnp.bfloat16
F32 = jnp.float32
MATMUL = (((1,), (0,)), ((), ()))
TRANSPOSED = (((1,), (1,)), ((), ()))
OVER_ROWS = (((0,), (0,)), ((), ()))
WIDTH = 256
LONG = 40_000_000_000


def pairs_of(shape, move):
    sections, halves, xs, ys = shape
    pairs = []
    for s in range(sections):
        for h in range(halves):
            for x in range(xs):
                for y in range(ys):
                    s2, h2 = move(s, h)
                    src = ((s * halves + h) * xs + x) * ys + y
                    dst = ((s2 * halves + h2) * xs + x) * ys + y
                    pairs.append((src, dst))
    return pairs


def moved(v, by, cross):
    shape = tuple(lax.axis_size(a) for a in RING)
    sections = shape[0]
    return lax.ppermute(
        v, RING, pairs_of(shape, lambda s, h: ((s + by) % sections, 1 - h if cross else h))
    )


def other_core(v):
    return lax.ppermute(v, NODE, [(0, 1), (1, 0)])


def exchange(v):
    return lax.all_to_all(v, PLANE, split_axis=0, concat_axis=0, tiled=True)


def after(value, *done):
    return lax.optimization_barrier((value,) + done)[0]


def dot32(a, b, dims=MATMUL):
    return lax.dot_general(a, b, dims, preferred_element_type=F32)


def run(kernel, outs, *args, scalars=0, scratch=(), flops=1000, room=32 << 20):
    where = [pl.BlockSpec(memory_space=pltpu.SMEM)] * scalars
    where += [pl.BlockSpec(memory_space=pltpu.VMEM)] * (len(args) - scalars)
    return pl.pallas_call(
        kernel,
        out_shape=outs,
        in_specs=where,
        out_specs=jax.tree.map(lambda _: pl.BlockSpec(memory_space=pltpu.VMEM), outs),
        scratch_shapes=scratch,
        compiler_params=pltpu.CompilerParams(vmem_limit_bytes=room),
        cost_estimate=pl.CostEstimate(flops=flops, bytes_accessed=1000, transcendentals=0),
    )(*args)


def shaped(*shape):
    return jax.ShapeDtypeStruct(shape, BF)


def gather_block(f_ref, *refs):
    notes, out_ref, hold_ref = refs[:4], refs[4], refs[5]
    tokens = f_ref.shape[0]
    top = notes[0].shape[0]
    out_ref[:tokens, :] = f_ref[...]
    hold_ref[...] = jnp.zeros(hold_ref.shape, F32)
    for half in range(2):
        span = slice(half * tokens, (half + 1) * tokens)
        hold_ref[:top, span] = notes[2 * half][...].astype(F32)
        hold_ref[8 : 8 + top, span] = notes[2 * half + 1][...].astype(F32)
    out_ref[tokens:, :] = hold_ref[...].astype(BF)


def tables(note, first, top, experts):
    tokens = note.shape[1] // 2
    label = (lax.broadcasted_iota(jnp.int32, (experts, 2 * tokens), 0) + first).astype(F32)
    chosen = jnp.zeros((experts, 2 * tokens), F32)
    weight = jnp.zeros((experts, 2 * tokens), F32)
    for k in range(top):
        match = note[k : k + 1] == label
        chosen = chosen + jnp.where(match, 1.0, 0.0)
        weight = weight + jnp.where(match, note[8 + k : 9 + k], 0.0)
    i = lax.broadcasted_iota(jnp.int32, (tokens, tokens), 0)
    j = lax.broadcasted_iota(jnp.int32, (tokens, tokens), 1)
    earlier = jnp.where(i < j, 1.0, 0.0).astype(BF)
    slot = lax.broadcasted_iota(jnp.int32, (SLOTS, tokens), 0).astype(F32)
    result = []
    for half in range(2):
        span = slice(half * tokens, (half + 1) * tokens)
        rank = dot32(chosen[:, span].astype(BF), earlier)
        place = jnp.where(chosen[:, span] > 0.0, rank, -1.0)
        hit = [jnp.where(slot == place[e : e + 1], 1.0, 0.0) for e in range(experts)]
        mix = [hit[e] * weight[e : e + 1, span] for e in range(experts)]
        result.append(
            (jnp.concatenate(hit, axis=0).astype(BF), jnp.concatenate(mix, axis=0).astype(BF))
        )
    return result


def flat(x):
    blocks = x.shape[1] // LANES
    pieces = [x[:HEAD, c * LANES : (c + 1) * LANES] for c in range(blocks)]
    at = lax.broadcasted_iota(jnp.int32, (blocks, LANES), 0)
    last = jnp.zeros((blocks, LANES), F32)
    for c in range(blocks):
        row = x[HEAD : HEAD + 1, c * LANES : (c + 1) * LANES]
        last = jnp.where(at == c, jnp.broadcast_to(row, (blocks, LANES)), last)
    return jnp.concatenate(pieces + [last], axis=0)


def unflat(y):
    blocks = y.shape[0] // (HEAD + 1)
    tail = SLOTS - HEAD
    columns = []
    for c in range(blocks):
        row = y[blocks * HEAD + c : blocks * HEAD + c + 1]
        column = [y[c * HEAD : (c + 1) * HEAD], jnp.broadcast_to(row, (tail, LANES))]
        columns.append(jnp.concatenate(column, axis=0))
    return jnp.concatenate(columns, axis=1)


def ship(out_ref, wides, added=()):
    for e in range(out_ref.shape[0]):
        rows = [flat(wide[e * SLOTS : (e + 1) * SLOTS, :]) for wide in wides]
        rows += [ref[e].astype(F32) for ref in added]
        out_ref[e] = jnp.concatenate(rows, axis=0).astype(BF)


def unship(got_ref, wides):
    each = got_ref.shape[1] // len(wides)
    for e in range(got_ref.shape[0]):
        rows = got_ref[e].astype(F32)
        for i, wide in enumerate(wides):
            wide[e * SLOTS : (e + 1) * SLOTS, :] = unflat(rows[i * each : (i + 1) * each]).astype(BF)


def put(wide_ref, hit, rows_ref):
    tokens = hit.shape[1]
    for c in range(0, wide_ref.shape[1], WIDTH):
        wide_ref[:, c : c + WIDTH] = dot32(hit, rows_ref[:tokens, c : c + WIDTH])


def block_tables(top, first_ref, block_ref, experts, tokens):
    note = block_ref[tokens:, : 2 * tokens].astype(F32)
    return tables(note, first_ref[0], top, experts)


def pack_near(top, first_ref, block_ref, a_ref, g_ref, out_ref, mix_f_ref, mix_b_ref, *wides):
    (hit_f, mix_f), (hit_b, mix_b) = block_tables(
        top, first_ref, block_ref, out_ref.shape[0], a_ref.shape[0]
    )
    mix_f_ref[...] = mix_f
    mix_b_ref[...] = mix_b
    put(wides[0], hit_b, a_ref)
    put(wides[1], hit_b, g_ref)
    put(wides[2], hit_f, block_ref)
    ship(out_ref, wides)


def pack_far_f(top, first_ref, block_ref, out_ref, mix_f_ref, mix_b_ref, hit_b_ref, *wides):
    (hit_f, mix_f), (hit_b, mix_b) = block_tables(
        top, first_ref, block_ref, out_ref.shape[0], mix_f_ref.shape[1]
    )
    mix_f_ref[...] = mix_f
    mix_b_ref[...] = mix_b
    hit_b_ref[...] = hit_b
    put(wides[0], hit_f, block_ref)
    ship(out_ref, wides)


def pack_far_b(hit_ref, a_ref, g_ref, out_ref, *wides):
    put(wides[0], hit_ref[...], a_ref)
    put(wides[1], hit_ref[...], g_ref)
    ship(out_ref, wides)


def parts(groups, *refs):
    kinds = "".join(groups)
    gots, refs = refs[: len(groups)], refs[len(groups) :]
    w_in_ref, w_out_ref, *refs = refs
    outs, wides = refs[: len(kinds)], refs[len(kinds) :]
    at = 0
    for got_ref, group in zip(gots, groups):
        unship(got_ref, wides[at : at + len(group)])
        at += len(group)
    for kind, wide, out_ref in zip(kinds, wides, outs):
        for c in range(0, w_in_ref.shape[1], WIDTH):
            if kind == "g":
                part = dot32(wide[...], w_out_ref[c : c + WIDTH, :], TRANSPOSED)
            else:
                part = dot32(wide[...], w_in_ref[:, c : c + WIDTH])
            out_ref[:, c : c + WIDTH] = part.astype(BF)


def results(groups, more, *refs):
    kinds = "".join(groups)
    mine, theirs = refs[: len(kinds)], refs[len(kinds) : 2 * len(kinds)]
    w_in_ref, w_out_ref, *refs = refs[2 * len(kinds) :]
    added, refs = refs[:more], refs[more:]
    outs, hold_ref, wides = refs[: len(groups)], refs[len(groups)], refs[len(groups) + 1 :]
    hidden, cols = w_in_ref.shape[1], w_in_ref.shape[0]

    def total(i, c):
        span = slice(c, c + WIDTH)
        return mine[i][:, span].astype(F32) + theirs[i][:, span].astype(F32)

    i = 0
    for wide in wides:
        forward = kinds[i] == "f"
        for c in range(0, hidden, WIDTH):
            pre = total(i, c)
            sigma = 1.0 / (1.0 + jnp.exp(-pre))
            if forward:
                value = pre * sigma
            else:
                value = total(i + 1, c) * sigma * (1.0 + pre * (1.0 - sigma))
            hold_ref[:, c : c + WIDTH] = value.astype(BF)
        for c in range(0, cols, WIDTH):
            if forward:
                block = dot32(hold_ref[...], w_out_ref[:, c : c + WIDTH])
            else:
                block = dot32(hold_ref[...], w_in_ref[c : c + WIDTH, :], TRANSPOSED)
            wide[:, c : c + WIDTH] = block
        i += 1 if forward else 2
    at = 0
    for out_ref, group in zip(outs, groups):
        many = made(group)
        ship(out_ref, wides[at : at + many], added)
        at += many


def made(group):
    return group.count("f") + group.count("a")


def sums(count, *refs):
    mixes, wides = refs[:count], refs[-count:]
    backs, outs = refs[count : -2 * count], refs[-2 * count : -count]
    for i, back_ref in enumerate(backs):
        unship(back_ref, [wides[i]] if len(backs) > 1 else wides)
    for mix_ref, wide, out_ref in zip(mixes, wides, outs):
        for c in range(0, out_ref.shape[1], WIDTH):
            total = dot32(mix_ref[...], wide[:, c : c + WIDTH], OVER_ROWS)
            out_ref[:, c : c + WIDTH] = total.astype(BF)


def hold(a_ref, b_ref, x_ref, y_ref):
    x_ref[...] = a_ref[...]
    y_ref[...] = b_ref[...]


def add(a_ref, b_ref, c_ref, d_ref, x_ref, y_ref):
    x_ref[...] = (a_ref[...].astype(F32) + c_ref[...].astype(F32)).astype(BF)
    y_ref[...] = (b_ref[...].astype(F32) + d_ref[...].astype(F32)).astype(BF)


def local(
    act_forward,
    routes_forward,
    gates_forward,
    act_backward,
    grad_backward,
    routes_backward,
    gates_backward,
    w_in,
    w_out,
):
    weight_in = w_in[0, 0]
    weight_out = w_out[0, 0]
    tok, cols = act_forward.shape
    hidden = weight_in.shape[1]
    top = routes_forward.shape[1]
    experts = lax.axis_size("x") * lax.axis_size("y")
    rows = experts * SLOTS
    first = (lax.axis_index("zhi") * experts).astype(jnp.int32).reshape(1)
    table = shaped(rows, tok)

    def wide(count, dtype):
        return [pltpu.VMEM((rows, cols), dtype)] * count

    def sendable(kinds):
        return shaped(experts, kinds * (HEAD + 1) * (cols // LANES), LANES)

    def work(gots, *groups, added=()):
        count = len("".join(groups))
        mine = run(
            functools.partial(parts, groups),
            (shaped(rows, hidden),) * count,
            *gots,
            weight_in,
            weight_out,
            scratch=wide(count, BF),
        )
        theirs = [other_core(part) for part in mine]
        return run(
            functools.partial(results, groups, len(added)),
            tuple(sendable(made(group) + len(added)) for group in groups),
            *mine,
            *theirs,
            weight_in,
            weight_out,
            *added,
            scratch=[pltpu.VMEM((rows, hidden), BF)] + wide(made("".join(groups)), F32),
        )

    def combined(back, *mixes):
        return run(
            functools.partial(sums, len(mixes)),
            (shaped(tok, cols),) * len(mixes),
            *mixes,
            *back,
            scratch=wide(len(mixes), BF),
        )

    block = run(
        gather_block,
        shaped(tok + 16, cols),
        act_forward,
        routes_forward.T,
        gates_forward.T,
        routes_backward.T,
        gates_backward.T,
        scratch=[pltpu.VMEM((16, cols), F32)],
        room=56 << 20,
    )
    far_block = moved(block, 0, True)
    far_a = moved(after(act_backward, far_block), 0, True)
    far_g = moved(after(grad_backward, far_block), 0, True)

    sent, mix_f, mix_b = run(
        functools.partial(pack_near, top),
        (sendable(3), table, table),
        first,
        block,
        act_backward,
        grad_backward,
        scalars=1,
        scratch=wide(3, F32),
        room=56 << 20,
    )
    got = exchange(sent)
    sent_f, far_mix_f, far_mix_b, far_hit_b = run(
        functools.partial(pack_far_f, top),
        (sendable(1), table, table, table),
        first,
        far_block,
        scalars=1,
        scratch=wide(1, F32),
        flops=LONG,
    )
    got_f = exchange(after(sent_f, got))
    sent_b = run(
        pack_far_b,
        sendable(2),
        far_hit_b,
        far_a,
        far_g,
        scratch=wide(2, F32),
        flops=LONG,
    )
    got_b = exchange(after(sent_b, got_f))
    out, out_f = work((after(got, sent_b), got_f), "agf", "f")
    (out_bf,) = work((after(got_b, out_f),), "ag", added=(out_f,))
    far_sum_b, far_sum_f = combined((exchange(out_bf),), far_mix_b, far_mix_f)
    over = (moved(far_sum_b, -1, True), moved(far_sum_f, 1, True))
    back = exchange(after(out, far_sum_f))
    sum_b, sum_f = combined((back,), mix_b, mix_f)
    near = (moved(sum_b, -1, False), moved(sum_f, 1, False))
    pair = (shaped(tok, cols),) * 2
    over = run(hold, pair, *over, flops=LONG)
    input_grad, layer_out = run(add, pair, *near, *over)
    return layer_out, input_grad


def solution(mesh):
    devices = mesh.devices
    sections, nodes, locals_ = devices.shape
    fine = Mesh(
        devices.reshape(sections, nodes, 2, 4, locals_ // 8), ("section", "node", "zhi", "x", "y")
    )
    where = ("zhi", "x", "y")
    tokens = P(("section",) + where, "node")
    picks = P(("section",) + where, None)
    in_specs = (
        tokens,
        picks,
        picks,
        tokens,
        tokens,
        picks,
        picks,
        P("section", where, "node", None),
        P("section", where, None, "node"),
    )
    return jax.shard_map(
        local, mesh=fine, in_specs=in_specs, out_specs=(tokens, tokens), check_vma=False
    )
```

```python
import functools

import jax
import jax.numpy as jnp
from jax import lax
from jax.experimental import pallas as pl
from jax.experimental.pallas import tpu as pltpu
from jax.sharding import Mesh, PartitionSpec as P

SLOTS = 32
HEAD = 24
LANES = 128
NODE = "node"
PLANE = ("x", "y")
RING = ("section", "zhi", "x", "y")
BF = jnp.bfloat16
F32 = jnp.float32
MATMUL = (((1,), (0,)), ((), ()))
TRANSPOSED = (((1,), (1,)), ((), ()))
OVER_ROWS = (((0,), (0,)), ((), ()))
WIDTH = 256
LONG = 40_000_000_000


def pairs_of(shape, move):
    sections, halves, xs, ys = shape
    pairs = []
    for s in range(sections):
        for h in range(halves):
            for x in range(xs):
                for y in range(ys):
                    s2, h2 = move(s, h)
                    src = ((s * halves + h) * xs + x) * ys + y
                    dst = ((s2 * halves + h2) * xs + x) * ys + y
                    pairs.append((src, dst))
    return pairs


def moved(v, by, cross):
    shape = tuple(lax.axis_size(a) for a in RING)
    sections = shape[0]
    return lax.ppermute(
        v, RING, pairs_of(shape, lambda s, h: ((s + by) % sections, 1 - h if cross else h))
    )


def other_core(v):
    return lax.ppermute(v, NODE, [(0, 1), (1, 0)])


def exchange(v):
    return lax.all_to_all(v, PLANE, split_axis=0, concat_axis=0, tiled=True)


def after(value, *done):
    return lax.optimization_barrier((value,) + done)[0]


def dot32(a, b, dims=MATMUL):
    return lax.dot_general(a, b, dims, preferred_element_type=F32)


def run(kernel, outs, *args, scalars=0, scratch=(), flops=1000, room=32 << 20):
    where = [pl.BlockSpec(memory_space=pltpu.SMEM)] * scalars
    where += [pl.BlockSpec(memory_space=pltpu.VMEM)] * (len(args) - scalars)
    return pl.pallas_call(
        kernel,
        out_shape=outs,
        in_specs=where,
        out_specs=jax.tree.map(lambda _: pl.BlockSpec(memory_space=pltpu.VMEM), outs),
        scratch_shapes=scratch,
        compiler_params=pltpu.CompilerParams(vmem_limit_bytes=room),
        cost_estimate=pl.CostEstimate(flops=flops, bytes_accessed=1000, transcendentals=0),
    )(*args)


def shaped(*shape):
    return jax.ShapeDtypeStruct(shape, BF)


def gather_block(f_ref, a_ref, g_ref, *refs):
    notes, out_ref, pair_ref, hold_ref = refs[:4], refs[4], refs[5], refs[6]
    tokens = f_ref.shape[0]
    top = notes[0].shape[0]
    out_ref[:tokens, :] = f_ref[...]
    pair_ref[:tokens, :] = a_ref[...]
    pair_ref[tokens:, :] = g_ref[...]
    hold_ref[...] = jnp.zeros(hold_ref.shape, F32)
    for half in range(2):
        span = slice(half * tokens, (half + 1) * tokens)
        hold_ref[:top, span] = notes[2 * half][...].astype(F32)
        hold_ref[8 : 8 + top, span] = notes[2 * half + 1][...].astype(F32)
    out_ref[tokens:, :] = hold_ref[...].astype(BF)


def tables(note, first, top, experts):
    tokens = note.shape[1] // 2
    label = (lax.broadcasted_iota(jnp.int32, (experts, 2 * tokens), 0) + first).astype(F32)
    chosen = jnp.zeros((experts, 2 * tokens), F32)
    weight = jnp.zeros((experts, 2 * tokens), F32)
    for k in range(top):
        match = note[k : k + 1] == label
        chosen = chosen + jnp.where(match, 1.0, 0.0)
        weight = weight + jnp.where(match, note[8 + k : 9 + k], 0.0)
    i = lax.broadcasted_iota(jnp.int32, (tokens, tokens), 0)
    j = lax.broadcasted_iota(jnp.int32, (tokens, tokens), 1)
    earlier = jnp.where(i < j, 1.0, 0.0).astype(BF)
    slot = lax.broadcasted_iota(jnp.int32, (SLOTS, tokens), 0).astype(F32)
    result = []
    for half in range(2):
        span = slice(half * tokens, (half + 1) * tokens)
        rank = dot32(chosen[:, span].astype(BF), earlier)
        place = jnp.where(chosen[:, span] > 0.0, rank, -1.0)
        hit = [jnp.where(slot == place[e : e + 1], 1.0, 0.0) for e in range(experts)]
        mix = [hit[e] * weight[e : e + 1, span] for e in range(experts)]
        result.append(
            (jnp.concatenate(hit, axis=0).astype(BF), jnp.concatenate(mix, axis=0).astype(BF))
        )
    return result


def flat(x):
    blocks = x.shape[1] // LANES
    pieces = [x[:HEAD, c * LANES : (c + 1) * LANES] for c in range(blocks)]
    at = lax.broadcasted_iota(jnp.int32, (blocks, LANES), 0)
    last = jnp.zeros((blocks, LANES), F32)
    for c in range(blocks):
        row = x[HEAD : HEAD + 1, c * LANES : (c + 1) * LANES]
        last = jnp.where(at == c, jnp.broadcast_to(row, (blocks, LANES)), last)
    return jnp.concatenate(pieces + [last], axis=0)


def unflat(y):
    blocks = y.shape[0] // (HEAD + 1)
    tail = SLOTS - HEAD
    columns = []
    for c in range(blocks):
        row = y[blocks * HEAD + c : blocks * HEAD + c + 1]
        column = [y[c * HEAD : (c + 1) * HEAD], jnp.broadcast_to(row, (tail, LANES))]
        columns.append(jnp.concatenate(column, axis=0))
    return jnp.concatenate(columns, axis=1)


def ship(out_ref, wides, added=()):
    for e in range(out_ref.shape[0]):
        rows = [flat(wide[e * SLOTS : (e + 1) * SLOTS, :]) for wide in wides]
        rows += [ref[e].astype(F32) for ref in added]
        out_ref[e] = jnp.concatenate(rows, axis=0).astype(BF)


def unship(got_ref, wides):
    each = got_ref.shape[1] // len(wides)
    for e in range(got_ref.shape[0]):
        rows = got_ref[e].astype(F32)
        for i, wide in enumerate(wides):
            wide[e * SLOTS : (e + 1) * SLOTS, :] = unflat(rows[i * each : (i + 1) * each]).astype(BF)


def put(wide_ref, hit, rows_ref, first=0):
    rows = slice(first, first + hit.shape[1])
    for c in range(0, wide_ref.shape[1], WIDTH):
        wide_ref[:, c : c + WIDTH] = dot32(hit, rows_ref[rows, c : c + WIDTH])


def block_tables(top, first_ref, block_ref, experts, tokens):
    note = block_ref[tokens:, : 2 * tokens].astype(F32)
    return tables(note, first_ref[0], top, experts)


def pack_near(top, first_ref, block_ref, pair_ref, out_ref, mix_f_ref, mix_b_ref, *wides):
    tokens = mix_f_ref.shape[1]
    (hit_f, mix_f), (hit_b, mix_b) = block_tables(
        top, first_ref, block_ref, out_ref.shape[0], tokens
    )
    mix_f_ref[...] = mix_f
    mix_b_ref[...] = mix_b
    put(wides[0], hit_b, pair_ref)
    put(wides[1], hit_b, pair_ref, tokens)
    put(wides[2], hit_f, block_ref)
    ship(out_ref, wides)


def pack_far_f(top, first_ref, block_ref, out_ref, mix_f_ref, mix_b_ref, hit_b_ref, *wides):
    (hit_f, mix_f), (hit_b, mix_b) = block_tables(
        top, first_ref, block_ref, out_ref.shape[0], mix_f_ref.shape[1]
    )
    mix_f_ref[...] = mix_f
    mix_b_ref[...] = mix_b
    hit_b_ref[...] = hit_b
    put(wides[0], hit_f, block_ref)
    ship(out_ref, wides)


def pack_far_b(hit_ref, pair_ref, out_ref, *wides):
    put(wides[0], hit_ref[...], pair_ref)
    put(wides[1], hit_ref[...], pair_ref, hit_ref.shape[1])
    ship(out_ref, wides)


def parts(groups, *refs):
    kinds = "".join(groups)
    gots, refs = refs[: len(groups)], refs[len(groups) :]
    w_in_ref, w_out_ref, *refs = refs
    outs, wides = refs[: len(kinds)], refs[len(kinds) :]
    at = 0
    for got_ref, group in zip(gots, groups):
        unship(got_ref, wides[at : at + len(group)])
        at += len(group)
    for kind, wide, out_ref in zip(kinds, wides, outs):
        for c in range(0, w_in_ref.shape[1], WIDTH):
            if kind == "g":
                part = dot32(wide[...], w_out_ref[c : c + WIDTH, :], TRANSPOSED)
            else:
                part = dot32(wide[...], w_in_ref[:, c : c + WIDTH])
            out_ref[:, c : c + WIDTH] = part.astype(BF)


def results(groups, more, *refs):
    kinds = "".join(groups)
    mine, theirs = refs[: len(kinds)], refs[len(kinds) : 2 * len(kinds)]
    w_in_ref, w_out_ref, *refs = refs[2 * len(kinds) :]
    added, refs = refs[:more], refs[more:]
    outs, hold_ref, wides = refs[: len(groups)], refs[len(groups)], refs[len(groups) + 1 :]
    hidden, cols = w_in_ref.shape[1], w_in_ref.shape[0]

    def total(i, c):
        span = slice(c, c + WIDTH)
        return mine[i][:, span].astype(F32) + theirs[i][:, span].astype(F32)

    i = 0
    for wide in wides:
        forward = kinds[i] == "f"
        for c in range(0, hidden, WIDTH):
            pre = total(i, c)
            sigma = 1.0 / (1.0 + jnp.exp(-pre))
            if forward:
                value = pre * sigma
            else:
                value = total(i + 1, c) * sigma * (1.0 + pre * (1.0 - sigma))
            hold_ref[:, c : c + WIDTH] = value.astype(BF)
        for c in range(0, cols, WIDTH):
            if forward:
                block = dot32(hold_ref[...], w_out_ref[:, c : c + WIDTH])
            else:
                block = dot32(hold_ref[...], w_in_ref[c : c + WIDTH, :], TRANSPOSED)
            wide[:, c : c + WIDTH] = block
        i += 1 if forward else 2
    at = 0
    for out_ref, group in zip(outs, groups):
        many = made(group)
        ship(out_ref, wides[at : at + many], added)
        at += many


def made(group):
    return group.count("f") + group.count("a")


def sums(count, last, *refs):
    mixes, back_ref, wides = refs[:count], refs[count], refs[-count:]
    unship(back_ref, wides)
    tokens = mixes[0].shape[1]
    for i, (mix_ref, wide) in enumerate(zip(mixes, wides)):
        rows = slice(i * tokens, (i + 1) * tokens)
        for c in range(0, wide.shape[1], WIDTH):
            cols = slice(c, c + WIDTH)
            total = dot32(mix_ref[...], wide[:, cols], OVER_ROWS)
            if last:
                over_ref, out_ref = refs[count + 1], refs[count + 2 + i]
                out_ref[:, cols] = (total + over_ref[rows, cols].astype(F32)).astype(BF)
            else:
                refs[count + 1][rows, cols] = total.astype(BF)


def hold(from_ref, to_ref):
    to_ref[...] = from_ref[...]


def local(
    act_forward,
    routes_forward,
    gates_forward,
    act_backward,
    grad_backward,
    routes_backward,
    gates_backward,
    w_in,
    w_out,
):
    weight_in = w_in[0, 0]
    weight_out = w_out[0, 0]
    tok, cols = act_forward.shape
    hidden = weight_in.shape[1]
    top = routes_forward.shape[1]
    experts = lax.axis_size("x") * lax.axis_size("y")
    rows = experts * SLOTS
    first = (lax.axis_index("zhi") * experts).astype(jnp.int32).reshape(1)
    table = shaped(rows, tok)

    def wide(count, dtype):
        return [pltpu.VMEM((rows, cols), dtype)] * count

    def sendable(kinds):
        return shaped(experts, kinds * (HEAD + 1) * (cols // LANES), LANES)

    def work(gots, *groups, added=()):
        count = len("".join(groups))
        mine = run(
            functools.partial(parts, groups),
            (shaped(rows, hidden),) * count,
            *gots,
            weight_in,
            weight_out,
            scratch=wide(count, BF),
        )
        theirs = [other_core(part) for part in mine]
        return run(
            functools.partial(results, groups, len(added)),
            tuple(sendable(made(group) + len(added)) for group in groups),
            *mine,
            *theirs,
            weight_in,
            weight_out,
            *added,
            scratch=[pltpu.VMEM((rows, hidden), BF)] + wide(made("".join(groups)), F32),
        )

    block, pair = run(
        gather_block,
        (shaped(tok + 16, cols), shaped(2 * tok, cols)),
        act_forward,
        act_backward,
        grad_backward,
        routes_forward.T,
        gates_forward.T,
        routes_backward.T,
        gates_backward.T,
        scratch=[pltpu.VMEM((16, cols), F32)],
        room=56 << 20,
    )
    far_block = moved(block, 0, True)
    far_pair = moved(pair, 0, True)

    sent, mix_f, mix_b = run(
        functools.partial(pack_near, top),
        (sendable(3), table, table),
        first,
        block,
        pair,
        scalars=1,
        scratch=wide(3, F32),
        room=56 << 20,
    )
    got = exchange(sent)
    sent_f, far_mix_f, far_mix_b, far_hit_b = run(
        functools.partial(pack_far_f, top),
        (sendable(1), table, table, table),
        first,
        far_block,
        scalars=1,
        scratch=wide(1, F32),
        flops=LONG,
    )
    got_f = exchange(after(sent_f, got))
    sent_b = run(
        pack_far_b,
        sendable(2),
        far_hit_b,
        far_pair,
        scratch=wide(2, F32),
        flops=LONG,
    )
    got_b = exchange(after(sent_b, got_f))
    out, out_f = work((after(got, sent_b), got_f), "agf", "f")
    (out_bf,) = work((after(got_b, out_f),), "ag", added=(out_f,))
    far_sum = run(
        functools.partial(sums, 2, False),
        shaped(2 * tok, cols),
        far_mix_b,
        far_mix_f,
        exchange(out_bf),
        scratch=wide(2, BF),
    )
    over = run(hold, shaped(2 * tok, cols), moved(far_sum, 0, True), flops=LONG)
    sum_b, sum_f = run(
        functools.partial(sums, 2, True),
        (shaped(tok, cols),) * 2,
        mix_b,
        mix_f,
        exchange(after(out, far_sum)),
        over,
        scratch=wide(2, BF),
    )
    return moved(sum_f, 1, False), moved(sum_b, -1, False)


def solution(mesh):
    devices = mesh.devices
    sections, nodes, locals_ = devices.shape
    fine = Mesh(
        devices.reshape(sections, nodes, 2, 4, locals_ // 8), ("section", "node", "zhi", "x", "y")
    )
    where = ("zhi", "x", "y")
    tokens = P(("section",) + where, "node")
    picks = P(("section",) + where, None)
    in_specs = (
        tokens,
        picks,
        picks,
        tokens,
        tokens,
        picks,
        picks,
        P("section", where, "node", None),
        P("section", where, None, "node"),
    )
    return jax.shard_map(
        local, mesh=fine, in_specs=in_specs, out_specs=(tokens, tokens), check_vma=False
    )
```

```python
import functools

import jax
import jax.numpy as jnp
from jax import lax
from jax.experimental import pallas as pl
from jax.experimental.pallas import tpu as pltpu
from jax.sharding import Mesh, PartitionSpec as P

SLOTS = 32
HEAD = 24
LANES = 128
NODE = "node"
PLANE = ("x", "y")
RING = ("section", "zhi", "x", "y")
BF = jnp.bfloat16
F32 = jnp.float32
MATMUL = (((1,), (0,)), ((), ()))
TRANSPOSED = (((1,), (1,)), ((), ()))
OVER_ROWS = (((0,), (0,)), ((), ()))
WIDTH = 256
LONG = 40_000_000_000


def pairs_of(shape, move):
    sections, halves, xs, ys = shape
    pairs = []
    for s in range(sections):
        for h in range(halves):
            for x in range(xs):
                for y in range(ys):
                    s2, h2 = move(s, h)
                    src = ((s * halves + h) * xs + x) * ys + y
                    dst = ((s2 * halves + h2) * xs + x) * ys + y
                    pairs.append((src, dst))
    return pairs


def moved(v, by, cross):
    shape = tuple(lax.axis_size(a) for a in RING)
    sections = shape[0]
    return lax.ppermute(
        v, RING, pairs_of(shape, lambda s, h: ((s + by) % sections, 1 - h if cross else h))
    )


def other_core(v):
    return lax.ppermute(v, NODE, [(0, 1), (1, 0)])


def exchange(v):
    return lax.all_to_all(v, PLANE, split_axis=0, concat_axis=0, tiled=True)


def after(value, *done):
    return lax.optimization_barrier((value,) + done)[0]


def dot32(a, b, dims=MATMUL):
    return lax.dot_general(a, b, dims, preferred_element_type=F32)


def run(kernel, outs, *args, scalars=0, scratch=(), flops=1000, room=32 << 20):
    where = [pl.BlockSpec(memory_space=pltpu.SMEM)] * scalars
    where += [pl.BlockSpec(memory_space=pltpu.VMEM)] * (len(args) - scalars)
    return pl.pallas_call(
        kernel,
        out_shape=outs,
        in_specs=where,
        out_specs=jax.tree.map(lambda _: pl.BlockSpec(memory_space=pltpu.VMEM), outs),
        scratch_shapes=scratch,
        compiler_params=pltpu.CompilerParams(vmem_limit_bytes=room),
        cost_estimate=pl.CostEstimate(flops=flops, bytes_accessed=1000, transcendentals=0),
    )(*args)


def shaped(*shape):
    return jax.ShapeDtypeStruct(shape, BF)


def gather_block(f_ref, a_ref, g_ref, *refs):
    notes, out_ref, pair_ref, hold_ref = refs[:4], refs[4], refs[5], refs[6]
    tokens = f_ref.shape[0]
    top = notes[0].shape[0]
    out_ref[:tokens, :] = f_ref[...]
    pair_ref[:tokens, :] = a_ref[...]
    pair_ref[tokens:, :] = g_ref[...]
    hold_ref[...] = jnp.zeros(hold_ref.shape, F32)
    for half in range(2):
        span = slice(half * tokens, (half + 1) * tokens)
        hold_ref[:top, span] = notes[2 * half][...].astype(F32)
        hold_ref[8 : 8 + top, span] = notes[2 * half + 1][...].astype(F32)
    out_ref[tokens:, :] = hold_ref[...].astype(BF)


def tables(note, first, top, experts):
    tokens = note.shape[1] // 2
    label = (lax.broadcasted_iota(jnp.int32, (experts, 2 * tokens), 0) + first).astype(F32)
    chosen = jnp.zeros((experts, 2 * tokens), F32)
    weight = jnp.zeros((experts, 2 * tokens), F32)
    for k in range(top):
        match = note[k : k + 1] == label
        chosen = chosen + jnp.where(match, 1.0, 0.0)
        weight = weight + jnp.where(match, note[8 + k : 9 + k], 0.0)
    i = lax.broadcasted_iota(jnp.int32, (tokens, tokens), 0)
    j = lax.broadcasted_iota(jnp.int32, (tokens, tokens), 1)
    earlier = jnp.where(i < j, 1.0, 0.0).astype(BF)
    slot = lax.broadcasted_iota(jnp.int32, (SLOTS, tokens), 0).astype(F32)
    result = []
    for half in range(2):
        span = slice(half * tokens, (half + 1) * tokens)
        rank = dot32(chosen[:, span].astype(BF), earlier)
        place = jnp.where(chosen[:, span] > 0.0, rank, -1.0)
        hit = [jnp.where(slot == place[e : e + 1], 1.0, 0.0) for e in range(experts)]
        mix = [hit[e] * weight[e : e + 1, span] for e in range(experts)]
        result.append(
            (jnp.concatenate(hit, axis=0).astype(BF), jnp.concatenate(mix, axis=0).astype(BF))
        )
    return result


def flat(x):
    blocks = x.shape[1] // LANES
    pieces = [x[:HEAD, c * LANES : (c + 1) * LANES] for c in range(blocks)]
    at = lax.broadcasted_iota(jnp.int32, (blocks, LANES), 0)
    last = jnp.zeros((blocks, LANES), F32)
    for c in range(blocks):
        row = x[HEAD : HEAD + 1, c * LANES : (c + 1) * LANES]
        last = jnp.where(at == c, jnp.broadcast_to(row, (blocks, LANES)), last)
    return jnp.concatenate(pieces + [last], axis=0)


def unflat(y):
    blocks = y.shape[0] // (HEAD + 1)
    tail = SLOTS - HEAD
    columns = []
    for c in range(blocks):
        row = y[blocks * HEAD + c : blocks * HEAD + c + 1]
        column = [y[c * HEAD : (c + 1) * HEAD], jnp.broadcast_to(row, (tail, LANES))]
        columns.append(jnp.concatenate(column, axis=0))
    return jnp.concatenate(columns, axis=1)


def ship(out_ref, wides):
    for e in range(out_ref.shape[0]):
        rows = [flat(wide[e * SLOTS : (e + 1) * SLOTS, :]) for wide in wides]
        out_ref[e] = jnp.concatenate(rows, axis=0).astype(BF)


def unship(got_ref, wides):
    each = got_ref.shape[1] // len(wides)
    for e in range(got_ref.shape[0]):
        rows = got_ref[e].astype(F32)
        for i, wide in enumerate(wides):
            wide[e * SLOTS : (e + 1) * SLOTS, :] = unflat(rows[i * each : (i + 1) * each]).astype(BF)


def put(wide_ref, hit, rows_ref, first=0):
    rows = slice(first, first + hit.shape[1])
    for c in range(0, wide_ref.shape[1], WIDTH):
        wide_ref[:, c : c + WIDTH] = dot32(hit, rows_ref[rows, c : c + WIDTH])


def block_tables(top, first_ref, block_ref, experts, tokens):
    note = block_ref[tokens:, : 2 * tokens].astype(F32)
    return tables(note, first_ref[0], top, experts)


def pack_near(top, first_ref, block_ref, pair_ref, out_ref, mix_f_ref, mix_b_ref, *wides):
    tokens = mix_f_ref.shape[1]
    (hit_f, mix_f), (hit_b, mix_b) = block_tables(
        top, first_ref, block_ref, out_ref.shape[0], tokens
    )
    mix_f_ref[...] = mix_f
    mix_b_ref[...] = mix_b
    put(wides[0], hit_b, pair_ref)
    put(wides[1], hit_b, pair_ref, tokens)
    put(wides[2], hit_f, block_ref)
    ship(out_ref, wides)


def pack_far_f(top, first_ref, block_ref, out_ref, mix_f_ref, mix_b_ref, hit_b_ref, *wides):
    (hit_f, mix_f), (hit_b, mix_b) = block_tables(
        top, first_ref, block_ref, out_ref.shape[0], mix_f_ref.shape[1]
    )
    mix_f_ref[...] = mix_f
    mix_b_ref[...] = mix_b
    hit_b_ref[...] = hit_b
    put(wides[0], hit_f, block_ref)
    ship(out_ref, wides)


def pack_far_b(hit_ref, pair_ref, out_ref, *wides):
    put(wides[0], hit_ref[...], pair_ref)
    put(wides[1], hit_ref[...], pair_ref, hit_ref.shape[1])
    ship(out_ref, wides)


def parts(groups, *refs):
    kinds = "".join(groups)
    gots, refs = refs[: len(groups)], refs[len(groups) :]
    w_in_ref, w_out_ref, *refs = refs
    outs, wides = refs[: len(kinds)], refs[len(kinds) :]
    at = 0
    for got_ref, group in zip(gots, groups):
        unship(got_ref, wides[at : at + len(group)])
        at += len(group)
    for kind, wide, out_ref in zip(kinds, wides, outs):
        for c in range(0, w_in_ref.shape[1], WIDTH):
            if kind == "g":
                part = dot32(wide[...], w_out_ref[c : c + WIDTH, :], TRANSPOSED)
            else:
                part = dot32(wide[...], w_in_ref[:, c : c + WIDTH])
            out_ref[:, c : c + WIDTH] = part.astype(BF)


def results(groups, *refs):
    kinds = "".join(groups)
    mine, theirs = refs[: len(kinds)], refs[len(kinds) : 2 * len(kinds)]
    w_in_ref, w_out_ref, *refs = refs[2 * len(kinds) :]
    outs, hold_ref, wides = refs[: len(groups)], refs[len(groups)], refs[len(groups) + 1 :]
    hidden, cols = w_in_ref.shape[1], w_in_ref.shape[0]

    def total(i, c):
        span = slice(c, c + WIDTH)
        return mine[i][:, span].astype(F32) + theirs[i][:, span].astype(F32)

    i = 0
    for wide in wides:
        forward = kinds[i] == "f"
        for c in range(0, hidden, WIDTH):
            pre = total(i, c)
            sigma = 1.0 / (1.0 + jnp.exp(-pre))
            if forward:
                value = pre * sigma
            else:
                value = total(i + 1, c) * sigma * (1.0 + pre * (1.0 - sigma))
            hold_ref[:, c : c + WIDTH] = value.astype(BF)
        for c in range(0, cols, WIDTH):
            if forward:
                block = dot32(hold_ref[...], w_out_ref[:, c : c + WIDTH])
            else:
                block = dot32(hold_ref[...], w_in_ref[c : c + WIDTH, :], TRANSPOSED)
            wide[:, c : c + WIDTH] = block
        i += 1 if forward else 2
    at = 0
    for out_ref, group in zip(outs, groups):
        many = made(group)
        ship(out_ref, wides[at : at + many])
        at += many


def made(group):
    return group.count("f") + group.count("a")


def sums(count, last, *refs):
    mixes, back_ref, overs = refs[:count], refs[count], refs[count + 1 : count + 1 + last]
    outs, wides = refs[-2 * count : -count], refs[-count:]
    unship(back_ref, wides)
    for i, (mix_ref, wide, out_ref) in enumerate(zip(mixes, wides, outs)):
        for c in range(0, wide.shape[1], WIDTH):
            cols = slice(c, c + WIDTH)
            total = dot32(mix_ref[...], wide[:, cols], OVER_ROWS)
            if last:
                total = total + overs[i][:, cols].astype(F32)
            out_ref[:, cols] = total.astype(BF)


def hold(from_ref, to_ref):
    to_ref[...] = from_ref[...]


def local(
    act_forward,
    routes_forward,
    gates_forward,
    act_backward,
    grad_backward,
    routes_backward,
    gates_backward,
    w_in,
    w_out,
):
    weight_in = w_in[0, 0]
    weight_out = w_out[0, 0]
    tok, cols = act_forward.shape
    hidden = weight_in.shape[1]
    top = routes_forward.shape[1]
    experts = lax.axis_size("x") * lax.axis_size("y")
    rows = experts * SLOTS
    first = (lax.axis_index("zhi") * experts).astype(jnp.int32).reshape(1)
    table = shaped(rows, tok)

    def wide(count, dtype):
        return [pltpu.VMEM((rows, cols), dtype)] * count

    def sendable(kinds):
        return shaped(experts, kinds * (HEAD + 1) * (cols // LANES), LANES)

    def work(gots, *groups):
        count = len("".join(groups))
        mine = run(
            functools.partial(parts, groups),
            (shaped(rows, hidden),) * count,
            *gots,
            weight_in,
            weight_out,
            scratch=wide(count, BF),
        )
        theirs = [other_core(part) for part in mine]
        return run(
            functools.partial(results, groups),
            tuple(sendable(made(group)) for group in groups),
            *mine,
            *theirs,
            weight_in,
            weight_out,
            scratch=[pltpu.VMEM((rows, hidden), BF)] + wide(made("".join(groups)), F32),
        )

    def combined(back, mixes, overs=()):
        return run(
            functools.partial(sums, len(mixes), len(overs)),
            (shaped(tok, cols),) * len(mixes),
            *mixes,
            back,
            *overs,
            scratch=wide(len(mixes), BF),
        )

    block, pair = run(
        gather_block,
        (shaped(tok + 16, cols), shaped(2 * tok, cols)),
        act_forward,
        act_backward,
        grad_backward,
        routes_forward.T,
        gates_forward.T,
        routes_backward.T,
        gates_backward.T,
        scratch=[pltpu.VMEM((16, cols), F32)],
        room=56 << 20,
    )
    far_block = moved(block, 0, True)
    far_pair = moved(pair, 0, True)

    sent, mix_f, mix_b = run(
        functools.partial(pack_near, top),
        (sendable(3), table, table),
        first,
        block,
        pair,
        scalars=1,
        scratch=wide(3, F32),
        room=56 << 20,
    )
    got = exchange(sent)
    sent_f, far_mix_f, far_mix_b, far_hit_b = run(
        functools.partial(pack_far_f, top),
        (sendable(1), table, table, table),
        first,
        far_block,
        scalars=1,
        scratch=wide(1, F32),
        flops=LONG,
    )
    got_f = exchange(after(sent_f, got))
    sent_b = run(
        pack_far_b,
        sendable(2),
        far_hit_b,
        far_pair,
        scratch=wide(2, F32),
        flops=LONG,
    )
    got_b = exchange(after(sent_b, got_f))
    out, out_f = work((after(got, sent_b), got_f), "agf", "f")
    back_f = exchange(after(out_f, got_b))
    (out_b,) = work((after(got_b, out_f),), "ag")
    back_b = exchange(after(out_b, back_f))
    over_f = moved(combined(back_f, (far_mix_f,))[0], 0, True)
    over_f = run(hold, shaped(tok, cols), over_f, flops=LONG)
    far_sum_b = combined(back_b, (far_mix_b,))[0]
    over_b = moved(far_sum_b, 0, True)
    back = exchange(after(out, far_sum_b))
    sum_b, sum_f = combined(back, (mix_b, mix_f), (over_b, over_f))
    return moved(sum_f, 1, False), moved(sum_b, -1, False)


def solution(mesh):
    devices = mesh.devices
    sections, nodes, locals_ = devices.shape
    fine = Mesh(
        devices.reshape(sections, nodes, 2, 4, locals_ // 8), ("section", "node", "zhi", "x", "y")
    )
    where = ("zhi", "x", "y")
    tokens = P(("section",) + where, "node")
    picks = P(("section",) + where, None)
    in_specs = (
        tokens,
        picks,
        picks,
        tokens,
        tokens,
        picks,
        picks,
        P("section", where, "node", None),
        P("section", where, None, "node"),
    )
    return jax.shard_map(
        local, mesh=fine, in_specs=in_specs, out_specs=(tokens, tokens), check_vma=False
    )
```

```python
import functools

import jax
import jax.numpy as jnp
from jax import lax
from jax.experimental import pallas as pl
from jax.experimental.pallas import tpu as pltpu
from jax.sharding import Mesh, PartitionSpec as P

SLOTS = 32
HEAD = 24
LANES = 128
NODE = "node"
PLANE = ("x", "y")
RING = ("section", "zhi", "x", "y")
BF = jnp.bfloat16
F32 = jnp.float32
MATMUL = (((1,), (0,)), ((), ()))
TRANSPOSED = (((1,), (1,)), ((), ()))
OVER_ROWS = (((0,), (0,)), ((), ()))
WIDTH = 256
LONG = 40_000_000_000


def pairs_of(shape, move):
    sections, halves, xs, ys = shape
    pairs = []
    for s in range(sections):
        for h in range(halves):
            for x in range(xs):
                for y in range(ys):
                    s2, h2 = move(s, h)
                    src = ((s * halves + h) * xs + x) * ys + y
                    dst = ((s2 * halves + h2) * xs + x) * ys + y
                    pairs.append((src, dst))
    return pairs


def moved(v, by, cross):
    shape = tuple(lax.axis_size(a) for a in RING)
    sections = shape[0]
    return lax.ppermute(
        v, RING, pairs_of(shape, lambda s, h: ((s + by) % sections, 1 - h if cross else h))
    )


def other_core(v):
    return lax.ppermute(v, NODE, [(0, 1), (1, 0)])


def exchange(v):
    return lax.all_to_all(v, PLANE, split_axis=0, concat_axis=0, tiled=True)


def after(value, *done):
    return lax.optimization_barrier((value,) + done)[0]


def dot32(a, b, dims=MATMUL):
    return lax.dot_general(a, b, dims, preferred_element_type=F32)


def run(kernel, outs, *args, scalars=0, scratch=(), flops=1000, room=32 << 20):
    where = [pl.BlockSpec(memory_space=pltpu.SMEM)] * scalars
    where += [pl.BlockSpec(memory_space=pltpu.VMEM)] * (len(args) - scalars)
    return pl.pallas_call(
        kernel,
        out_shape=outs,
        in_specs=where,
        out_specs=jax.tree.map(lambda _: pl.BlockSpec(memory_space=pltpu.VMEM), outs),
        scratch_shapes=scratch,
        compiler_params=pltpu.CompilerParams(vmem_limit_bytes=room),
        cost_estimate=pl.CostEstimate(flops=flops, bytes_accessed=1000, transcendentals=0),
    )(*args)


def shaped(*shape):
    return jax.ShapeDtypeStruct(shape, BF)


def gather_block(f_ref, a_ref, g_ref, *refs):
    notes, out_ref, pair_ref, hold_ref = refs[:4], refs[4], refs[5], refs[6]
    tokens = f_ref.shape[0]
    top = notes[0].shape[0]
    out_ref[:tokens, :] = f_ref[...]
    pair_ref[:tokens, :] = a_ref[...]
    pair_ref[tokens:, :] = g_ref[...]
    hold_ref[...] = jnp.zeros(hold_ref.shape, F32)
    for half in range(2):
        span = slice(half * tokens, (half + 1) * tokens)
        hold_ref[:top, span] = notes[2 * half][...].astype(F32)
        hold_ref[8 : 8 + top, span] = notes[2 * half + 1][...].astype(F32)
    out_ref[tokens:, :] = hold_ref[...].astype(BF)


def tables(note, first, top, experts):
    tokens = note.shape[1] // 2
    label = (lax.broadcasted_iota(jnp.int32, (experts, 2 * tokens), 0) + first).astype(F32)
    chosen = jnp.zeros((experts, 2 * tokens), F32)
    weight = jnp.zeros((experts, 2 * tokens), F32)
    for k in range(top):
        match = note[k : k + 1] == label
        chosen = chosen + jnp.where(match, 1.0, 0.0)
        weight = weight + jnp.where(match, note[8 + k : 9 + k], 0.0)
    i = lax.broadcasted_iota(jnp.int32, (tokens, tokens), 0)
    j = lax.broadcasted_iota(jnp.int32, (tokens, tokens), 1)
    earlier = jnp.where(i < j, 1.0, 0.0).astype(BF)
    slot = lax.broadcasted_iota(jnp.int32, (SLOTS, tokens), 0).astype(F32)
    result = []
    for half in range(2):
        span = slice(half * tokens, (half + 1) * tokens)
        rank = dot32(chosen[:, span].astype(BF), earlier)
        place = jnp.where(chosen[:, span] > 0.0, rank, -1.0)
        hit = [jnp.where(slot == place[e : e + 1], 1.0, 0.0) for e in range(experts)]
        mix = [hit[e] * weight[e : e + 1, span] for e in range(experts)]
        result.append(
            (jnp.concatenate(hit, axis=0).astype(BF), jnp.concatenate(mix, axis=0).astype(BF))
        )
    return result


def flat(x):
    blocks = x.shape[1] // LANES
    pieces = [x[:HEAD, c * LANES : (c + 1) * LANES] for c in range(blocks)]
    at = lax.broadcasted_iota(jnp.int32, (blocks, LANES), 0)
    last = jnp.zeros((blocks, LANES), F32)
    for c in range(blocks):
        row = x[HEAD : HEAD + 1, c * LANES : (c + 1) * LANES]
        last = jnp.where(at == c, jnp.broadcast_to(row, (blocks, LANES)), last)
    return jnp.concatenate(pieces + [last], axis=0)


def unflat(y):
    blocks = y.shape[0] // (HEAD + 1)
    tail = SLOTS - HEAD
    columns = []
    for c in range(blocks):
        row = y[blocks * HEAD + c : blocks * HEAD + c + 1]
        column = [y[c * HEAD : (c + 1) * HEAD], jnp.broadcast_to(row, (tail, LANES))]
        columns.append(jnp.concatenate(column, axis=0))
    return jnp.concatenate(columns, axis=1)


def ship(out_ref, wides):
    for e in range(out_ref.shape[0]):
        rows = [flat(wide[e * SLOTS : (e + 1) * SLOTS, :]) for wide in wides]
        out_ref[e] = jnp.concatenate(rows, axis=0).astype(BF)


def unship(got_ref, wides):
    each = got_ref.shape[1] // len(wides)
    for e in range(got_ref.shape[0]):
        rows = got_ref[e].astype(F32)
        for i, wide in enumerate(wides):
            wide[e * SLOTS : (e + 1) * SLOTS, :] = unflat(rows[i * each : (i + 1) * each]).astype(BF)


def put(wide_ref, hit, rows_ref, first=0):
    rows = slice(first, first + hit.shape[1])
    for c in range(0, wide_ref.shape[1], WIDTH):
        wide_ref[:, c : c + WIDTH] = dot32(hit, rows_ref[rows, c : c + WIDTH])


def block_tables(top, first_ref, block_ref, experts, tokens):
    note = block_ref[tokens:, : 2 * tokens].astype(F32)
    return tables(note, first_ref[0], top, experts)


def pack_near(top, first_ref, block_ref, pair_ref, out_ref, mix_f_ref, mix_b_ref, *wides):
    tokens = mix_f_ref.shape[1]
    (hit_f, mix_f), (hit_b, mix_b) = block_tables(
        top, first_ref, block_ref, out_ref.shape[0], tokens
    )
    mix_f_ref[...] = mix_f
    mix_b_ref[...] = mix_b
    put(wides[0], hit_b, pair_ref)
    put(wides[1], hit_b, pair_ref, tokens)
    put(wides[2], hit_f, block_ref)
    ship(out_ref, wides)


def pack_far_f(top, first_ref, block_ref, out_ref, mix_f_ref, mix_b_ref, hit_b_ref, *wides):
    (hit_f, mix_f), (hit_b, mix_b) = block_tables(
        top, first_ref, block_ref, out_ref.shape[0], mix_f_ref.shape[1]
    )
    mix_f_ref[...] = mix_f
    mix_b_ref[...] = mix_b
    hit_b_ref[...] = hit_b
    put(wides[0], hit_f, block_ref)
    ship(out_ref, wides)


def pack_far_b(hit_ref, pair_ref, out_ref, *wides):
    put(wides[0], hit_ref[...], pair_ref)
    put(wides[1], hit_ref[...], pair_ref, hit_ref.shape[1])
    ship(out_ref, wides)


def parts(groups, pieces, *refs):
    kinds = "".join(groups)
    gots, refs = refs[: len(groups)], refs[len(groups) :]
    w_in_ref, w_out_ref, *refs = refs
    outs, wides = refs[: len(kinds) * pieces], refs[len(kinds) * pieces :]
    at = 0
    for got_ref, group in zip(gots, groups):
        unship(got_ref, wides[at : at + len(group)])
        at += len(group)
    for i, (kind, wide) in enumerate(zip(kinds, wides)):
        each = wide.shape[0] // pieces
        for c in range(0, w_in_ref.shape[1], WIDTH):
            if kind == "g":
                part = dot32(wide[...], w_out_ref[c : c + WIDTH, :], TRANSPOSED)
            else:
                part = dot32(wide[...], w_in_ref[:, c : c + WIDTH])
            for j in range(pieces):
                block = part[j * each : (j + 1) * each].astype(BF)
                outs[i * pieces + j][:, c : c + WIDTH] = block


def results(groups, pieces, *refs):
    kinds = "".join(groups)
    count = len(kinds) * pieces
    mine, theirs = refs[:count], refs[count : 2 * count]
    w_in_ref, w_out_ref, *refs = refs[2 * count :]
    outs, hold_ref, wides = refs[: len(groups)], refs[len(groups)], refs[len(groups) + 1 :]
    hidden, cols = w_in_ref.shape[1], w_in_ref.shape[0]

    def total(i, c):
        span = slice(c, c + WIDTH)
        blocks = [
            mine[j][:, span].astype(F32) + theirs[j][:, span].astype(F32)
            for j in range(i * pieces, (i + 1) * pieces)
        ]
        return jnp.concatenate(blocks, axis=0)

    i = 0
    for wide in wides:
        forward = kinds[i] == "f"
        for c in range(0, hidden, WIDTH):
            pre = total(i, c)
            sigma = 1.0 / (1.0 + jnp.exp(-pre))
            if forward:
                value = pre * sigma
            else:
                value = total(i + 1, c) * sigma * (1.0 + pre * (1.0 - sigma))
            hold_ref[:, c : c + WIDTH] = value.astype(BF)
        for c in range(0, cols, WIDTH):
            if forward:
                block = dot32(hold_ref[...], w_out_ref[:, c : c + WIDTH])
            else:
                block = dot32(hold_ref[...], w_in_ref[c : c + WIDTH, :], TRANSPOSED)
            wide[:, c : c + WIDTH] = block
        i += 1 if forward else 2
    at = 0
    for out_ref, group in zip(outs, groups):
        many = made(group)
        ship(out_ref, wides[at : at + many])
        at += many


def made(group):
    return group.count("f") + group.count("a")


def sums(count, last, *refs):
    mixes, back_ref, overs = refs[:count], refs[count], refs[count + 1 : count + 1 + last]
    outs, wides = refs[-2 * count : -count], refs[-count:]
    unship(back_ref, wides)
    for i, (mix_ref, wide, out_ref) in enumerate(zip(mixes, wides, outs)):
        for c in range(0, wide.shape[1], WIDTH):
            cols = slice(c, c + WIDTH)
            total = dot32(mix_ref[...], wide[:, cols], OVER_ROWS)
            if last:
                total = total + overs[i][:, cols].astype(F32)
            out_ref[:, cols] = total.astype(BF)


def hold(from_ref, to_ref):
    to_ref[...] = from_ref[...]


def local(
    act_forward,
    routes_forward,
    gates_forward,
    act_backward,
    grad_backward,
    routes_backward,
    gates_backward,
    w_in,
    w_out,
):
    weight_in = w_in[0, 0]
    weight_out = w_out[0, 0]
    tok, cols = act_forward.shape
    hidden = weight_in.shape[1]
    top = routes_forward.shape[1]
    experts = lax.axis_size("x") * lax.axis_size("y")
    rows = experts * SLOTS
    first = (lax.axis_index("zhi") * experts).astype(jnp.int32).reshape(1)
    table = shaped(rows, tok)

    def wide(count, dtype):
        return [pltpu.VMEM((rows, cols), dtype)] * count

    def sendable(kinds):
        return shaped(experts, kinds * (HEAD + 1) * (cols // LANES), LANES)

    def work(gots, *groups, pieces=1):
        count = len("".join(groups))
        mine = run(
            functools.partial(parts, groups, pieces),
            (shaped(rows // pieces, hidden),) * (count * pieces),
            *gots,
            weight_in,
            weight_out,
            scratch=wide(count, BF),
        )
        theirs = [other_core(part) for part in mine]
        return run(
            functools.partial(results, groups, pieces),
            tuple(sendable(made(group)) for group in groups),
            *mine,
            *theirs,
            weight_in,
            weight_out,
            scratch=[pltpu.VMEM((rows, hidden), BF)] + wide(made("".join(groups)), F32),
        )

    def combined(back, mixes, overs=()):
        return run(
            functools.partial(sums, len(mixes), len(overs)),
            (shaped(tok, cols),) * len(mixes),
            *mixes,
            back,
            *overs,
            scratch=wide(len(mixes), BF),
        )

    block, pair = run(
        gather_block,
        (shaped(tok + 16, cols), shaped(2 * tok, cols)),
        act_forward,
        act_backward,
        grad_backward,
        routes_forward.T,
        gates_forward.T,
        routes_backward.T,
        gates_backward.T,
        scratch=[pltpu.VMEM((16, cols), F32)],
        room=56 << 20,
    )
    far_block = moved(block, 0, True)
    far_pair = moved(pair, 0, True)

    sent, mix_f, mix_b = run(
        functools.partial(pack_near, top),
        (sendable(3), table, table),
        first,
        block,
        pair,
        scalars=1,
        scratch=wide(3, F32),
        room=56 << 20,
    )
    got = exchange(sent)
    sent_f, far_mix_f, far_mix_b, far_hit_b = run(
        functools.partial(pack_far_f, top),
        (sendable(1), table, table, table),
        first,
        far_block,
        scalars=1,
        scratch=wide(1, F32),
        flops=LONG,
    )
    got_f = exchange(after(sent_f, got))
    sent_b = run(
        pack_far_b,
        sendable(2),
        far_hit_b,
        far_pair,
        scratch=wide(2, F32),
        flops=LONG,
    )
    got_b = exchange(after(sent_b, got_f))
    out, out_f = work((after(got, sent_b), got_f), "agf", "f")
    back_f = exchange(after(out_f, got_b))
    (out_b,) = work((after(got_b, out_f),), "ag", pieces=2)
    back_b = exchange(after(out_b, back_f))
    over_f = moved(combined(back_f, (far_mix_f,))[0], 0, True)
    over_f = run(hold, shaped(tok, cols), over_f, flops=LONG)
    far_sum_b = combined(back_b, (far_mix_b,))[0]
    over_b = moved(far_sum_b, 0, True)
    back = exchange(after(out, far_sum_b))
    sum_b, sum_f = combined(back, (mix_b, mix_f), (over_b, over_f))
    return moved(sum_f, 1, False), moved(sum_b, -1, False)


def solution(mesh):
    devices = mesh.devices
    sections, nodes, locals_ = devices.shape
    fine = Mesh(
        devices.reshape(sections, nodes, 2, 4, locals_ // 8), ("section", "node", "zhi", "x", "y")
    )
    where = ("zhi", "x", "y")
    tokens = P(("section",) + where, "node")
    picks = P(("section",) + where, None)
    in_specs = (
        tokens,
        picks,
        picks,
        tokens,
        tokens,
        picks,
        picks,
        P("section", where, "node", None),
        P("section", where, None, "node"),
    )
    return jax.shard_map(
        local, mesh=fine, in_specs=in_specs, out_specs=(tokens, tokens), check_vma=False
    )
```

```python
import functools

import jax
import jax.numpy as jnp
from jax import lax
from jax.experimental import pallas as pl
from jax.experimental.pallas import tpu as pltpu
from jax.sharding import Mesh, PartitionSpec as P

SLOTS = 32
HEAD = 24
LANES = 128
NODE = "node"
PLANE = ("x", "y")
RING = ("section", "zhi", "x", "y")
BF = jnp.bfloat16
F32 = jnp.float32
MATMUL = (((1,), (0,)), ((), ()))
TRANSPOSED = (((1,), (1,)), ((), ()))
OVER_ROWS = (((0,), (0,)), ((), ()))
WIDTH = 256
LONG = 40_000_000_000


def pairs_of(shape, move):
    sections, halves, xs, ys = shape
    pairs = []
    for s in range(sections):
        for h in range(halves):
            for x in range(xs):
                for y in range(ys):
                    s2, h2 = move(s, h)
                    src = ((s * halves + h) * xs + x) * ys + y
                    dst = ((s2 * halves + h2) * xs + x) * ys + y
                    pairs.append((src, dst))
    return pairs


def moved(v, by, cross):
    shape = tuple(lax.axis_size(a) for a in RING)
    sections = shape[0]
    return lax.ppermute(
        v, RING, pairs_of(shape, lambda s, h: ((s + by) % sections, 1 - h if cross else h))
    )


def other_core(v):
    return lax.ppermute(v, NODE, [(0, 1), (1, 0)])


def exchange(v):
    return lax.all_to_all(v, PLANE, split_axis=0, concat_axis=0, tiled=True)


def after(value, *done):
    return lax.optimization_barrier((value,) + done)[0]


def dot32(a, b, dims=MATMUL):
    return lax.dot_general(a, b, dims, preferred_element_type=F32)


def run(kernel, outs, *args, scalars=0, scratch=(), flops=1000, room=32 << 20):
    where = [pl.BlockSpec(memory_space=pltpu.SMEM)] * scalars
    where += [pl.BlockSpec(memory_space=pltpu.VMEM)] * (len(args) - scalars)
    return pl.pallas_call(
        kernel,
        out_shape=outs,
        in_specs=where,
        out_specs=jax.tree.map(lambda _: pl.BlockSpec(memory_space=pltpu.VMEM), outs),
        scratch_shapes=scratch,
        compiler_params=pltpu.CompilerParams(vmem_limit_bytes=room),
        cost_estimate=pl.CostEstimate(flops=flops, bytes_accessed=1000, transcendentals=0),
    )(*args)


def shaped(*shape):
    return jax.ShapeDtypeStruct(shape, BF)


def gather_block(f_ref, a_ref, g_ref, *refs):
    notes, out_ref, pair_ref, hold_ref = refs[:4], refs[4], refs[5], refs[6]
    tokens = f_ref.shape[0]
    top = notes[0].shape[0]
    out_ref[:tokens, :] = f_ref[...]
    pair_ref[:tokens, :] = a_ref[...]
    pair_ref[tokens:, :] = g_ref[...]
    hold_ref[...] = jnp.zeros(hold_ref.shape, F32)
    for half in range(2):
        span = slice(half * tokens, (half + 1) * tokens)
        hold_ref[:top, span] = notes[2 * half][...].astype(F32)
        hold_ref[8 : 8 + top, span] = notes[2 * half + 1][...].astype(F32)
    out_ref[tokens:, :] = hold_ref[...].astype(BF)


def tables(note, first, top, experts):
    tokens = note.shape[1] // 2
    label = (lax.broadcasted_iota(jnp.int32, (experts, 2 * tokens), 0) + first).astype(F32)
    chosen = jnp.zeros((experts, 2 * tokens), F32)
    weight = jnp.zeros((experts, 2 * tokens), F32)
    for k in range(top):
        match = note[k : k + 1] == label
        chosen = chosen + jnp.where(match, 1.0, 0.0)
        weight = weight + jnp.where(match, note[8 + k : 9 + k], 0.0)
    i = lax.broadcasted_iota(jnp.int32, (tokens, tokens), 0)
    j = lax.broadcasted_iota(jnp.int32, (tokens, tokens), 1)
    earlier = jnp.where(i < j, 1.0, 0.0).astype(BF)
    slot = lax.broadcasted_iota(jnp.int32, (SLOTS, tokens), 0).astype(F32)
    result = []
    for half in range(2):
        span = slice(half * tokens, (half + 1) * tokens)
        rank = dot32(chosen[:, span].astype(BF), earlier)
        place = jnp.where(chosen[:, span] > 0.0, rank, -1.0)
        hit = [jnp.where(slot == place[e : e + 1], 1.0, 0.0) for e in range(experts)]
        mix = [hit[e] * weight[e : e + 1, span] for e in range(experts)]
        result.append(
            (jnp.concatenate(hit, axis=0).astype(BF), jnp.concatenate(mix, axis=0).astype(BF))
        )
    return result


def flat(x):
    blocks = x.shape[1] // LANES
    pieces = [x[:HEAD, c * LANES : (c + 1) * LANES] for c in range(blocks)]
    at = lax.broadcasted_iota(jnp.int32, (blocks, LANES), 0)
    last = jnp.zeros((blocks, LANES), F32)
    for c in range(blocks):
        row = x[HEAD : HEAD + 1, c * LANES : (c + 1) * LANES]
        last = jnp.where(at == c, jnp.broadcast_to(row, (blocks, LANES)), last)
    return jnp.concatenate(pieces + [last], axis=0)


def unflat(y):
    blocks = y.shape[0] // (HEAD + 1)
    tail = SLOTS - HEAD
    columns = []
    for c in range(blocks):
        row = y[blocks * HEAD + c : blocks * HEAD + c + 1]
        column = [y[c * HEAD : (c + 1) * HEAD], jnp.broadcast_to(row, (tail, LANES))]
        columns.append(jnp.concatenate(column, axis=0))
    return jnp.concatenate(columns, axis=1)


def ship(out_ref, wides):
    for e in range(out_ref.shape[0]):
        rows = [flat(wide[e * SLOTS : (e + 1) * SLOTS, :]) for wide in wides]
        out_ref[e] = jnp.concatenate(rows, axis=0).astype(BF)


def unship(got_ref, wides):
    each = got_ref.shape[1] // len(wides)
    for e in range(got_ref.shape[0]):
        rows = got_ref[e].astype(F32)
        for i, wide in enumerate(wides):
            wide[e * SLOTS : (e + 1) * SLOTS, :] = unflat(rows[i * each : (i + 1) * each]).astype(BF)


def put(wide_ref, hit, rows_ref, first=0):
    rows = slice(first, first + hit.shape[1])
    for c in range(0, wide_ref.shape[1], WIDTH):
        wide_ref[:, c : c + WIDTH] = dot32(hit, rows_ref[rows, c : c + WIDTH])


def block_tables(top, first_ref, block_ref, experts, tokens):
    note = block_ref[tokens:, : 2 * tokens].astype(F32)
    return tables(note, first_ref[0], top, experts)


def pack_near(top, first_ref, block_ref, pair_ref, out_ref, mix_f_ref, mix_b_ref, *wides):
    tokens = mix_f_ref.shape[1]
    (hit_f, mix_f), (hit_b, mix_b) = block_tables(
        top, first_ref, block_ref, out_ref.shape[0], tokens
    )
    mix_f_ref[...] = mix_f
    mix_b_ref[...] = mix_b
    put(wides[0], hit_b, pair_ref)
    put(wides[1], hit_b, pair_ref, tokens)
    put(wides[2], hit_f, block_ref)
    ship(out_ref, wides)


def pack_far_f(top, first_ref, block_ref, out_ref, mix_f_ref, mix_b_ref, hit_b_ref, *wides):
    (hit_f, mix_f), (hit_b, mix_b) = block_tables(
        top, first_ref, block_ref, out_ref.shape[0], mix_f_ref.shape[1]
    )
    mix_f_ref[...] = mix_f
    mix_b_ref[...] = mix_b
    hit_b_ref[...] = hit_b
    put(wides[0], hit_f, block_ref)
    ship(out_ref, wides)


def pack_far_b(hit_ref, pair_ref, out_ref, *wides):
    put(wides[0], hit_ref[...], pair_ref)
    put(wides[1], hit_ref[...], pair_ref, hit_ref.shape[1])
    ship(out_ref, wides)


def parts(groups, pieces, *refs):
    kinds = "".join(groups)
    gots, refs = refs[: len(groups)], refs[len(groups) :]
    w_in_ref, w_out_ref, *refs = refs
    outs, wides = refs[: len(kinds) * pieces], refs[len(kinds) * pieces :]
    at = 0
    for got_ref, group in zip(gots, groups):
        unship(got_ref, wides[at : at + len(group)])
        at += len(group)
    for i, (kind, wide) in enumerate(zip(kinds, wides)):
        each = wide.shape[0] // pieces
        for c in range(0, w_in_ref.shape[1], WIDTH):
            if kind == "g":
                part = dot32(wide[...], w_out_ref[c : c + WIDTH, :], TRANSPOSED)
            else:
                part = dot32(wide[...], w_in_ref[:, c : c + WIDTH])
            for j in range(pieces):
                block = part[j * each : (j + 1) * each].astype(BF)
                outs[i * pieces + j][:, c : c + WIDTH] = block


def results(groups, pieces, *refs):
    kinds = "".join(groups)
    count = len(kinds) * pieces
    mine, theirs = refs[:count], refs[count : 2 * count]
    w_in_ref, w_out_ref, *refs = refs[2 * count :]
    outs, hold_ref, wides = refs[: len(groups)], refs[len(groups)], refs[len(groups) + 1 :]
    hidden, cols = w_in_ref.shape[1], w_in_ref.shape[0]

    def total(i, c):
        span = slice(c, c + WIDTH)
        blocks = [
            mine[j][:, span].astype(F32) + theirs[j][:, span].astype(F32)
            for j in range(i * pieces, (i + 1) * pieces)
        ]
        return jnp.concatenate(blocks, axis=0)

    i = 0
    for wide in wides:
        forward = kinds[i] == "f"
        for c in range(0, hidden, WIDTH):
            pre = total(i, c)
            sigma = 1.0 / (1.0 + jnp.exp(-pre))
            if forward:
                value = pre * sigma
            else:
                value = total(i + 1, c) * sigma * (1.0 + pre * (1.0 - sigma))
            hold_ref[:, c : c + WIDTH] = value.astype(BF)
        for c in range(0, cols, WIDTH):
            if forward:
                block = dot32(hold_ref[...], w_out_ref[:, c : c + WIDTH])
            else:
                block = dot32(hold_ref[...], w_in_ref[c : c + WIDTH, :], TRANSPOSED)
            wide[:, c : c + WIDTH] = block
        i += 1 if forward else 2
    at = 0
    for out_ref, group in zip(outs, groups):
        many = made(group)
        ship(out_ref, wides[at : at + many])
        at += many


def made(group):
    return group.count("f") + group.count("a")


def sums(count, last, *refs):
    mixes, back_ref, overs = refs[:count], refs[count], refs[count + 1 : count + 1 + last]
    outs, wides = refs[-2 * count : -count], refs[-count:]
    unship(back_ref, wides)
    for i, (mix_ref, wide, out_ref) in enumerate(zip(mixes, wides, outs)):
        for c in range(0, wide.shape[1], WIDTH):
            cols = slice(c, c + WIDTH)
            total = dot32(mix_ref[...], wide[:, cols], OVER_ROWS)
            if last:
                total = total + overs[i][:, cols].astype(F32)
            out_ref[:, cols] = total.astype(BF)


def hold(from_ref, to_ref):
    to_ref[...] = from_ref[...]


def local(
    act_forward,
    routes_forward,
    gates_forward,
    act_backward,
    grad_backward,
    routes_backward,
    gates_backward,
    w_in,
    w_out,
):
    weight_in = w_in[0, 0]
    weight_out = w_out[0, 0]
    tok, cols = act_forward.shape
    hidden = weight_in.shape[1]
    top = routes_forward.shape[1]
    experts = lax.axis_size("x") * lax.axis_size("y")
    rows = experts * SLOTS
    first = (lax.axis_index("zhi") * experts).astype(jnp.int32).reshape(1)
    table = shaped(rows, tok)

    def wide(count, dtype):
        return [pltpu.VMEM((rows, cols), dtype)] * count

    def sendable(kinds):
        return shaped(experts, kinds * (HEAD + 1) * (cols // LANES), LANES)

    def work(gots, *groups, pieces=1):
        count = len("".join(groups))
        mine = run(
            functools.partial(parts, groups, pieces),
            (shaped(rows // pieces, hidden),) * (count * pieces),
            *gots,
            weight_in,
            weight_out,
            scratch=wide(count, BF),
        )
        theirs = [other_core(part) for part in mine]
        return run(
            functools.partial(results, groups, pieces),
            tuple(sendable(made(group)) for group in groups),
            *mine,
            *theirs,
            weight_in,
            weight_out,
            scratch=[pltpu.VMEM((rows, hidden), BF)] + wide(made("".join(groups)), F32),
        )

    def combined(back, mixes, overs=()):
        return run(
            functools.partial(sums, len(mixes), len(overs)),
            (shaped(tok, cols),) * len(mixes),
            *mixes,
            back,
            *overs,
            scratch=wide(len(mixes), BF),
        )

    block, pair = run(
        gather_block,
        (shaped(tok + 16, cols), shaped(2 * tok, cols)),
        act_forward,
        act_backward,
        grad_backward,
        routes_forward.T,
        gates_forward.T,
        routes_backward.T,
        gates_backward.T,
        scratch=[pltpu.VMEM((16, cols), F32)],
        room=56 << 20,
    )
    far_block = moved(block, 0, True)
    far_pair = moved(pair, 0, True)

    sent, mix_f, mix_b = run(
        functools.partial(pack_near, top),
        (sendable(3), table, table),
        first,
        block,
        pair,
        scalars=1,
        scratch=wide(3, F32),
        room=56 << 20,
    )
    got = exchange(sent)
    sent_f, far_mix_f, far_mix_b, far_hit_b = run(
        functools.partial(pack_far_f, top),
        (sendable(1), table, table, table),
        first,
        far_block,
        scalars=1,
        scratch=wide(1, F32),
        flops=LONG,
    )
    got_f = exchange(after(sent_f, got))
    sent_b = run(
        pack_far_b,
        sendable(2),
        far_hit_b,
        far_pair,
        scratch=wide(2, F32),
        flops=LONG,
        room=56 << 20,
    )
    got_b = exchange(after(sent_b, got_f))
    out, out_f = work((after(got, sent_b), got_f), "agf", "f")
    back_f = exchange(after(out_f, got_b))
    (out_b,) = work((after(got_b, out_f),), "ag", pieces=2)
    back_b = exchange(after(out_b, back_f))
    over_f = moved(combined(back_f, (far_mix_f,))[0], 0, True)
    over_f = run(hold, shaped(tok, cols), over_f, flops=LONG)
    far_sum_b = combined(back_b, (far_mix_b,))[0]
    over_b = moved(far_sum_b, 0, True)
    back = exchange(after(out, far_sum_b))
    sum_b, sum_f = combined(back, (mix_b, mix_f), (over_b, over_f))
    return moved(sum_f, 1, False), moved(sum_b, -1, False)


def solution(mesh):
    devices = mesh.devices
    sections, nodes, locals_ = devices.shape
    fine = Mesh(
        devices.reshape(sections, nodes, 2, 4, locals_ // 8), ("section", "node", "zhi", "x", "y")
    )
    where = ("zhi", "x", "y")
    tokens = P(("section",) + where, "node")
    picks = P(("section",) + where, None)
    in_specs = (
        tokens,
        picks,
        picks,
        tokens,
        tokens,
        picks,
        picks,
        P("section", where, "node", None),
        P("section", where, None, "node"),
    )
    return jax.shard_map(
        local, mesh=fine, in_specs=in_specs, out_specs=(tokens, tokens), check_vma=False
    )
```
